256 devices in a mesh: dp: 64 (over y, x_lo, z), tensor: 4 (over x_hi, core).
Axes of the slice: x: 4 (x_hi: 2, x_lo: 2; x = x_hi * 2 + x_lo), y: 4, z: 8, core: 2. Of those that a mesh axis runs over, the one named last changes fastest.
Arguments:
- hidden: bfloat16 [128, 2, 256, 4096], P('dp', None, None, 'tensor'), may hold values from -6 to 6
- lengths: int32 [128, 2], P('dp'), may hold values from 1 to 256, as said below
- norm_gain: float32 [4096], replicated, may hold values from 0.25 to 1.75
- q_norm_gain: float32 [128], replicated, may hold values from 0.5 to 2
- k_norm_gain: float32 [128], replicated, may hold values from 0.5 to 2
- query_weight: bfloat16 [4096, 4096], P('dp', 'tensor'), may hold values from -0.09375 to 0.09375
- key_weight: bfloat16 [4096, 1024], P('dp', 'tensor'), may hold values from -0.09375 to 0.09375
- value_weight: bfloat16 [4096, 1024], P('dp', 'tensor'), may hold values from -0.09375 to 0.09375
Outputs:
- embeddings: bfloat16 [128, 2, 4096], P('dp', None, 'tensor')
- pair_loss: float32 [128], P('dp')
- loss: float32 [], replicated
The draws below stay inside these ranges and needn't reach their ends.
Inputs may be any that keep to these rules, and one draw needn't show every extreme that they name: `lengths`: every token slot below the length is valid; some passage has all 256 slots valid.
All inputs are finite; a program needn't handle non-finite values.
Results may differ from the reference program's by a relative error of at most 0.0071.
The reference program's roundings to bfloat16 on the way (of `normed`, `query_heads` and `attn_weights`) count: a program that leaves them out, or rounds other values in their place, can miss the bound.
Values may be sent and summed in bfloat16 or wider, within the bound.
No kernel may reach another device: no remote copies, remote signals or barrier semaphores. Data moves between devices by JAX's collectives and lax.ppermute only.
A program may use at most 128 MiB of HBM per device.

```python
import math
import jax
import jax.numpy as jnp
from jax import lax

D = 4096
HEADS = 32
KV_HEADS = 8
HEAD_DIM = 128
SEQ_LEN = 256
PAIRS = 128


def draw_lengths(key, part):
    key = jax.random.fold_in(key, 11)
    drawn = jax.random.randint(key, (PAIRS, 2), 1, SEQ_LEN + 1, dtype=jnp.int32)
    return drawn.at[0, 1].set(SEQ_LEN)


def steps_of(rng, dims, cuts, low, high):
    def one(axis_at, parts):
        steps = jax.random.uniform(jax.random.fold_in(jax.random.fold_in(rng, 6), axis_at), (parts,), jnp.float32, low / len(cuts), high / len(cuts))
        return jnp.repeat(jnp.exp(steps), dims[axis_at] // parts).reshape((-1,) + (1,) * (len(dims) - axis_at - 1))

    level = one(*cuts[0])
    for cut in cuts[1:]:
        level = level * one(*cut)
    return level


def noise(key, extent, width, limit, split=(), held_as=jnp.bfloat16):
    values = jax.random.normal(key, extent, jnp.float32) * width
    if len(split) > 0:
        values = steps_of(key, extent, split, -0.22, 0.18) * values
    return jnp.clip(values, min=-limit, max=limit).astype(held_as)


def setup_inputs(seed: int = 0) -> dict:
    streams_of = jax.random.split(jax.random.key(seed), 9)
    return {
        "hidden": noise(streams_of[0], (PAIRS, 2, SEQ_LEN, D), 1.0, 6.0, ((0, 64), (3, 4))),
        "lengths": draw_lengths(jax.random.fold_in(streams_of[8], 71), 0),
        "norm_gain": jnp.clip(1.0 + 0.15 * jax.random.normal(streams_of[2], (D,), jnp.float32), 0.25, 1.75),
        "q_norm_gain": jnp.clip(jnp.exp(jax.random.uniform(streams_of[3], (HEAD_DIM,), jnp.float32, math.log(0.5), math.log(2.0))), 0.5, 2.0),
        "k_norm_gain": jnp.clip(jnp.exp(jax.random.uniform(streams_of[4], (HEAD_DIM,), jnp.float32, math.log(0.5), math.log(2.0))), 0.5, 2.0),
        "query_weight": noise(streams_of[5], (D, HEADS * HEAD_DIM), D ** -0.5, 0.09375, ((0, 64), (1, 4))),
        "key_weight": noise(streams_of[6], (D, KV_HEADS * HEAD_DIM), D ** -0.5, 0.09375, ((0, 64), (1, 4))),
        "value_weight": noise(streams_of[7], (D, KV_HEADS * HEAD_DIM), D ** -0.5, 0.09375, ((0, 64), (1, 4))),
    }


EPS = 1e-06
SCORE_SCALE = 20.0

def rms_rows(values):
    return values * lax.rsqrt(lax.optimization_barrier(jnp.mean(values * values, axis=-1, keepdims=True)) + EPS)

def attend(query_proj, key_proj, value_proj, seq_lengths, q_norm_gain, k_norm_gain):
    seq_count, seq_slots, kv_local, head_size = key_proj.shape
    query_heads = (rms_rows(query_proj.reshape(seq_count, kv_local, -1, head_size)) * q_norm_gain).astype(jnp.bfloat16)
    key_heads = (rms_rows(key_proj) * k_norm_gain).astype(jnp.bfloat16)
    value_heads = value_proj.astype(jnp.bfloat16)
    scores = jnp.einsum('skgd,slkd->skgl', query_heads.astype(jnp.float32), key_heads.astype(jnp.float32)) / math.sqrt(head_size)
    positions = jnp.arange(seq_slots, dtype=jnp.int32)
    valid = positions[None, :] < seq_lengths[:, None]
    scores = jnp.where(valid[:, None, None, :], scores, -1e+30)
    peak = lax.optimization_barrier(jnp.max(scores, axis=-1, keepdims=True))
    expo = jnp.exp(scores - peak)
    attn_weights = (expo / lax.optimization_barrier(jnp.sum(expo, axis=-1, keepdims=True))).astype(jnp.bfloat16)
    mixed = jnp.einsum('skgl,slkd->skgd', attn_weights.astype(jnp.float32), value_heads.astype(jnp.float32))
    return mixed.reshape(seq_count, -1)

def reference(hidden, lengths, norm_gain, q_norm_gain, k_norm_gain, query_weight, key_weight, value_weight):

    def embed_pair(inputs):
        hidden_pair, pair_lengths = inputs
        flat_rows = hidden_pair.reshape(-1, D).astype(jnp.float32)
        normed = (rms_rows(flat_rows) * norm_gain).astype(jnp.bfloat16)
        key_proj = jnp.dot(normed, key_weight, preferred_element_type=jnp.float32).reshape(2, SEQ_LEN, KV_HEADS, HEAD_DIM)
        value_proj = jnp.dot(normed, value_weight, preferred_element_type=jnp.float32).reshape(2, SEQ_LEN, KV_HEADS, HEAD_DIM)
        last_rows = normed.reshape(2, SEQ_LEN, D)[jnp.arange(2, dtype=jnp.int32), (pair_lengths - 1).astype(jnp.int32)]
        query_proj = jnp.dot(last_rows, query_weight, preferred_element_type=jnp.float32)
        mixed = attend(query_proj, key_proj, value_proj, pair_lengths, q_norm_gain, k_norm_gain)
        scale_back = lax.rsqrt(lax.optimization_barrier(jnp.sum(mixed * mixed, axis=-1, keepdims=True)) + EPS)
        return (mixed * scale_back).astype(jnp.bfloat16)
    embeddings = lax.map(embed_pair, (hidden, lengths))
    query_emb = embeddings[:, 0]
    passage_emb = embeddings[:, 1]
    sim = SCORE_SCALE * jnp.dot(query_emb, passage_emb.T, preferred_element_type=jnp.float32)
    row_lse = jax.nn.logsumexp(sim, axis=1)
    col_lse = jax.nn.logsumexp(sim, axis=0)
    positive = SCORE_SCALE * lax.optimization_barrier(jnp.sum(query_emb.astype(jnp.float32) * passage_emb.astype(jnp.float32), axis=-1))
    pair_loss = 0.5 * (row_lse + col_lse) - positive
    loss = jnp.mean(pair_loss)
    return (embeddings, pair_loss, loss)
```

```python
import math

import jax
import jax.numpy as jnp
from jax import lax
from jax.experimental import pallas as pl
from jax.experimental.pallas import tpu as pltpu
from jax.sharding import PartitionSpec as P

HEAD_DIM = 128
EPS = 1e-06
SCORE_SCALE = 20.0

Y, XLO, Z = 4, 2, 8
XHI, CORES = 2, 2
GROUPS = Y * XLO
Z_GROUPS = [[g * Z + z for z in range(Z)] for g in range(GROUPS)]


def rms_rows(values):
    return values * lax.rsqrt(jnp.mean(values * values, axis=-1, keepdims=True) + EPS)


def shift(array, dx=0, dy=0, dz=0):
    pairs = []
    for y in range(Y):
        for x in range(XHI * XLO):
            for z in range(Z):
                for core in range(CORES):

                    def at(x, y, z):
                        x_hi, x_lo = divmod(x, XLO)
                        dp = (y * XLO + x_lo) * Z + z
                        return dp * (XHI * CORES) + x_hi * CORES + core

                    there = at((x + dx) % (XHI * XLO), (y + dy) % Y, (z + dz) % Z)
                    pairs.append((at(x, y, z), there))
    return lax.ppermute(array, ("dp", "tensor"), pairs)


def swap_tensor(array, mask):
    size = XHI * CORES
    return lax.ppermute(array, "tensor", [(i, i ^ mask) for i in range(size)])


def swap_x_lo(array):
    pairs = [(i, (i // Z ^ 1) * Z + i % Z) for i in range(GROUPS * Z)]
    return lax.ppermute(array, "dp", pairs)


def exchange(chunks, groups):
    return lax.all_to_all(
        chunks, "dp", split_axis=0, concat_axis=0, tiled=True, axis_index_groups=groups
    )


def last_rows_kernel(at_ref, r0, r1, r2, r3, gain_ref, out_ref, raw_ref, row_ref):
    y_at, x_lo_at, tensor_at = at_ref[0], at_ref[1], at_ref[2]
    refs = [r0, r1, r2, r3]
    seq_count, width = r0.shape
    rows = width // (XLO * Z)
    squares = None
    for k, ref in enumerate(refs):
        x = ref[...].astype(jnp.float32)
        raw_ref[k] = x
        part = jnp.sum(x * x, axis=-1, keepdims=True)
        squares = part if squares is None else squares + part
    scale = lax.rsqrt(squares / (len(refs) * width) + EPS)
    row_ref[...] = jnp.zeros_like(row_ref)
    for step in range(Y):
        slice_at = (y_at + step) & (Y - 1)
        normed = raw_ref[slice_at ^ tensor_at] * scale * gain_ref[pl.ds(slice_at, 1), :]
        normed = normed.astype(jnp.bfloat16).astype(jnp.float32)
        halves = [normed[:, : Z * rows], normed[:, Z * rows :]]
        row, lane = (0, step * XLO * rows) if step < Y - 1 else (8, 0)
        for x in range(XLO):
            half = jnp.where(x_lo_at == x, halves[0], halves[1])
            for z in range(Z):
                at = lane + x * rows
                row_ref[z, row : row + seq_count, at : at + rows] = half[
                    :, z * rows : (z + 1) * rows
                ]
    out_ref[...] = row_ref[...].astype(jnp.bfloat16)


def query_kernel(rows_ref, w0, w1, w2, w3, out_ref, acc_ref):
    depth, _ = w0.shape
    rows = rows_ref[...].astype(jnp.float32)
    total = None
    for step, w_ref in enumerate([w0, w1, w2, w3]):
        row, lane = (0, step * depth) if step < Y - 1 else (8, 0)
        lhs = rows[:, row : row + 8, lane : lane + depth].reshape(Z * 8, depth)
        part = jnp.dot(
            lhs.astype(jnp.bfloat16), w_ref[:, HEAD_DIM:], preferred_element_type=jnp.float32
        )
        total = part if total is None else total + part
    high = total.astype(jnp.bfloat16).astype(jnp.float32)
    low = (total - high).astype(jnp.bfloat16).astype(jnp.float32)
    both = high + pltpu.roll(low, 4, 0)
    for head in range(both.shape[1] // HEAD_DIM):
        block = both[:, head * HEAD_DIM : (head + 1) * HEAD_DIM]
        acc_ref[:, head * 8 : (head + 1) * 8, :] = block.reshape(Z, 8, HEAD_DIM)
    out_ref[...] = acc_ref[...].astype(jnp.bfloat16)


def kv_attend_kernel(
    at_ref,
    len_ref,
    x0_ref,
    x1_ref,
    x2_ref,
    x3_ref,
    own_ref,
    up_ref,
    far_ref,
    down_ref,
    last_ref,
    gain_ref,
    qg_ref,
    kg_ref,
    out_ref,
    wk_ref,
    wv_ref,
    query_ref,
):
    x_refs = [x0_ref, x1_ref, x2_ref, x3_ref]
    _, slots, width = x0_ref.shape
    slices = len(x_refs)
    rows = width // (XLO * Z)
    seq = pl.program_id(0)
    heads = out_ref.shape[1]
    y_at, x_lo_at, tensor_at = at_ref[0], at_ref[1], at_ref[2]

    @pl.when(seq == 0)
    def _():
        for step, piece in enumerate([own_ref, up_ref, far_ref, down_ref]):
            base = ((y_at + step) & (Y - 1)) * width
            for x in range(XLO):
                half = base + (x_lo_at ^ x) * (Z * rows)
                for z in range(Z):
                    at = pl.ds(pl.multiple_of(half + z * rows, rows), rows)
                    block = slice(x * rows, (x + 1) * rows)
                    wk_ref[at, :] = piece[z, block, : 2 * HEAD_DIM]
                    wv_ref[at, :HEAD_DIM] = piece[z, block, 2 * HEAD_DIM :]
                    start = (step * XLO + x) * rows
                    wv_ref[at, HEAD_DIM:] = last_ref[z, start : start + rows, :]
        parts = last_ref[:, Y * XLO * rows :, :].astype(jnp.float32)
        parts = jnp.sum(parts, axis=0)
        query_ref[...] = parts + pltpu.roll(parts, parts.shape[0] - 4, 0)

    squares = None
    for k in range(slices):
        x = x_refs[k][0].astype(jnp.float32)
        part = jnp.sum(x * x, axis=-1, keepdims=True)
        squares = part if squares is None else squares + part
    scale = lax.rsqrt(squares / (slices * width) + EPS)
    key_proj = value_proj = None
    for k in range(slices):
        x = x_refs[k][0].astype(jnp.float32)
        slice_at = tensor_at ^ k
        normed = (x * scale * gain_ref[pl.ds(slice_at, 1), :]).astype(jnp.bfloat16)
        at = pl.ds(pl.multiple_of(slice_at * width, width), width)
        kp = jnp.dot(normed, wk_ref[at, :], preferred_element_type=jnp.float32)
        vp = jnp.dot(normed, wv_ref[at, :], preferred_element_type=jnp.float32)
        key_proj = kp if key_proj is None else key_proj + kp
        value_proj = vp if value_proj is None else value_proj + vp
    query = query_ref[pl.ds(seq, heads, stride=8), :]
    query = (rms_rows(query) * qg_ref[...]).astype(jnp.bfloat16)
    first = lax.broadcasted_iota(jnp.int32, (heads, 1), 0) < heads // 2
    scores = []
    for h in range(2):
        key = key_proj[:, h * HEAD_DIM : (h + 1) * HEAD_DIM]
        key = (rms_rows(key) * kg_ref[...]).astype(jnp.bfloat16)
        scores.append(
            lax.dot_general(
                query, key, (((1,), (1,)), ((), ())), preferred_element_type=jnp.float32
            )
        )
    scores = jnp.where(first, scores[0], scores[1]) / math.sqrt(HEAD_DIM)
    positions = lax.broadcasted_iota(jnp.int32, (1, slots), 1)
    scores = jnp.where(positions < len_ref[seq], scores, -1e30)
    expo = jnp.exp(scores - jnp.max(scores, axis=-1, keepdims=True))
    weights = (expo / jnp.sum(expo, axis=-1, keepdims=True)).astype(jnp.bfloat16)
    value = value_proj.astype(jnp.bfloat16)
    mixed = jnp.dot(weights, value, preferred_element_type=jnp.float32)
    out_ref[0] = jnp.where(first, mixed[:, :HEAD_DIM], mixed[:, HEAD_DIM:])


SMEM = pl.BlockSpec(memory_space=pltpu.SMEM)
VMEM = pl.BlockSpec(memory_space=pltpu.VMEM)


def last_rows_call(at, raw, gains):
    seq_count, width = raw[0].shape
    shape = (Z, 16, (Y - 1) * XLO * (width // (XLO * Z)))
    return pl.pallas_call(
        last_rows_kernel,
        in_specs=[SMEM] + [VMEM] * (len(raw) + 1),
        out_specs=VMEM,
        out_shape=jax.ShapeDtypeStruct(shape, jnp.bfloat16),
        scratch_shapes=[
            pltpu.VMEM((len(raw), seq_count, width), jnp.float32),
            pltpu.VMEM(shape, jnp.float32),
        ],
    )(at, *raw, gains)


def query_call(z_own, rest):
    shape = (Z, (rest[0].shape[1] // HEAD_DIM - 1) * 8, HEAD_DIM)
    tail = z_own.shape[1] // 16 - 1
    return pl.pallas_call(
        query_kernel,
        grid=(1,),
        in_specs=[pl.BlockSpec((Z, 16, z_own.shape[2]), lambda i: (0, tail, 0))]
        + [VMEM] * len(rest),
        out_specs=VMEM,
        out_shape=jax.ShapeDtypeStruct(shape, jnp.bfloat16),
        scratch_shapes=[pltpu.VMEM(shape, jnp.float32)],
    )(z_own, *rest)


def kv_attend(at, lengths, slices, pieces, last, gains, heads, qg, kg):
    seq_count, slots, width = slices[0].shape
    model_width = gains.size
    kv_width = 2 * HEAD_DIM
    x_spec = pl.BlockSpec((1, slots, width), lambda seq: (seq, 0, 0))
    return pl.pallas_call(
        kv_attend_kernel,
        grid=(seq_count,),
        in_specs=[SMEM, SMEM] + [x_spec] * len(slices) + [VMEM] * (len(pieces) + 4),
        out_specs=pl.BlockSpec((1, heads, HEAD_DIM), lambda seq: (seq, 0, 0)),
        out_shape=jax.ShapeDtypeStruct((seq_count, heads, HEAD_DIM), jnp.float32),
        scratch_shapes=[pltpu.VMEM((model_width, kv_width), jnp.bfloat16)] * 2
        + [pltpu.VMEM((heads * 8, HEAD_DIM), jnp.float32)],
        compiler_params=pltpu.CompilerParams(vmem_limit_bytes=40 * 1024 * 1024),
        cost_estimate=pl.CostEstimate(
            flops=4 * seq_count * slots * model_width * kv_width,
            bytes_accessed=2 * seq_count * slots * model_width + 4 * model_width * kv_width,
            transcendentals=seq_count * heads * slots,
        ),
    )(at, lengths, *slices, *pieces, last, gains, qg, kg)


def body(
    hidden, lengths, norm_gain, q_norm_gain, k_norm_gain, query_weight, key_weight, value_weight
):
    tensor_size = lax.axis_size("tensor")
    tensor_at = lax.axis_index("tensor")
    dp_at = lax.axis_index("dp")
    x_lo_at = (dp_at >> (Z.bit_length() - 1)) & (XLO - 1)
    y_at = dp_at >> ((Z * XLO).bit_length() - 1)
    at = jnp.stack([y_at, x_lo_at, tensor_at]).astype(jnp.int32)

    pair_count, _, seq_slots, width_local = hidden.shape
    seq_count = 2 * pair_count
    own = hidden.reshape(seq_count, seq_slots, width_local)
    seq_lengths = lengths.reshape(-1)
    rows_local, kv_width = key_weight.shape
    query_width = query_weight.shape[1]
    gains = norm_gain.reshape(tensor_size, width_local)

    kv_weight = jnp.concatenate([key_weight, value_weight], axis=1)
    kv_both = jnp.concatenate([kv_weight, swap_x_lo(kv_weight)])
    query_other = swap_x_lo(query_weight)
    last_own = jnp.take_along_axis(own, (seq_lengths - 1)[:, None, None], axis=1)[:, 0]
    last_raw = [last_own] + [swap_tensor(last_own, k) for k in range(1, tensor_size)]

    peer = swap_tensor(own, 1)
    sent_own = lax.optimization_barrier((own, kv_both, query_other, *last_raw))[0]
    far = swap_tensor(sent_own, 2)

    block = kv_both[:, : kv_width + HEAD_DIM]
    rows = last_rows_call(at, last_raw, gains)
    z_own = exchange(
        jnp.concatenate([jnp.broadcast_to(block[None], (Z,) + block.shape), rows], axis=1),
        Z_GROUPS,
    )
    pieces = [z_own] + [shift(z_own, dy=-step) for step in range(1, Y)]

    rest = jnp.concatenate(
        [kv_both[:, kv_width + HEAD_DIM :], jnp.concatenate([query_weight, query_other])], axis=1
    )
    rest = [rest] + [shift(rest, dy=-step) for step in range(1, Y)]
    partial_q = query_call(z_own, rest)
    head = jnp.concatenate([array[:, :HEAD_DIM] for array in rest])
    last = exchange(
        jnp.concatenate([jnp.broadcast_to(head[None], (Z,) + head.shape), partial_q], axis=1),
        Z_GROUPS,
    )
    far_peer = swap_tensor(lax.optimization_barrier((far, last, *pieces))[0], 1)

    mixed = kv_attend(
        at,
        seq_lengths,
        [own, peer, far, far_peer],
        pieces,
        last,
        gains,
        query_width // HEAD_DIM,
        q_norm_gain[None],
        k_norm_gain[None],
    ).reshape(seq_count, width_local)

    sent = mixed.astype(jnp.bfloat16)
    every = exchange(jnp.broadcast_to(sent[None], (GROUPS * Z,) + sent.shape), None)
    every = every.reshape(-1, 2, width_local)
    dots = jnp.dot(every[:, 0], every[:, 1].T, preferred_element_type=jnp.float32)
    every_f32 = every.astype(jnp.float32)
    norms = jnp.sum(every_f32 * every_f32, axis=-1).T
    part = jnp.concatenate([dots, norms], axis=0)
    parts = [part] + [swap_tensor(part, k) for k in range(1, tensor_size)]
    total = (parts[0] + parts[1]) + (parts[2] + parts[3])
    pairs = dots.shape[0]
    scales = lax.rsqrt(total[pairs:] + EPS)
    sim = SCORE_SCALE * total[:pairs] * scales[0][:, None] * scales[1][None, :]
    row_lse = jax.nn.logsumexp(sim, axis=1)
    col_lse = jax.nn.logsumexp(sim, axis=0)
    positive = jnp.sum(jnp.where(jnp.eye(pairs, dtype=bool), sim, 0.0), axis=0)
    all_loss = 0.5 * (row_lse + col_lse) - positive
    loss = jnp.mean(all_loss)
    pair_loss = lax.dynamic_slice_in_dim(all_loss, dp_at * pair_count, pair_count)
    own_scale = lax.dynamic_slice_in_dim(scales, dp_at * pair_count, pair_count, axis=1)
    embeddings = (mixed.reshape(pair_count, 2, width_local) * own_scale.T[:, :, None]).astype(
        jnp.bfloat16
    )
    return (embeddings, pair_loss, loss)


def solution(mesh):
    in_specs = (
        P("dp", None, None, "tensor"),
        P("dp", None),
        P(),
        P(),
        P(),
        P("dp", "tensor"),
        P("dp", "tensor"),
        P("dp", "tensor"),
    )
    out_specs = (P("dp", None, "tensor"), P("dp"), P())
    return jax.shard_map(body, mesh=mesh, in_specs=in_specs, out_specs=out_specs, check_vma=False)
```

```python
import math

import jax
import jax.numpy as jnp
from jax import lax
from jax.experimental import pallas as pl
from jax.experimental.pallas import tpu as pltpu
from jax.sharding import PartitionSpec as P

HEAD_DIM = 128
EPS = 1e-06
SCORE_SCALE = 20.0

Y, XLO, Z = 4, 2, 8
XHI, CORES = 2, 2
GROUPS = Y * XLO
Z_GROUPS = [[g * Z + z for z in range(Z)] for g in range(GROUPS)]


def rms_rows(values):
    return values * lax.rsqrt(jnp.mean(values * values, axis=-1, keepdims=True) + EPS)


def shift(array, dx=0, dy=0, dz=0):
    pairs = []
    for y in range(Y):
        for x in range(XHI * XLO):
            for z in range(Z):
                for core in range(CORES):

                    def at(x, y, z):
                        x_hi, x_lo = divmod(x, XLO)
                        dp = (y * XLO + x_lo) * Z + z
                        return dp * (XHI * CORES) + x_hi * CORES + core

                    there = at((x + dx) % (XHI * XLO), (y + dy) % Y, (z + dz) % Z)
                    pairs.append((at(x, y, z), there))
    return lax.ppermute(array, ("dp", "tensor"), pairs)


def swap_tensor(array, mask):
    size = XHI * CORES
    return lax.ppermute(array, "tensor", [(i, i ^ mask) for i in range(size)])


def swap_x_lo(array):
    pairs = [(i, (i // Z ^ 1) * Z + i % Z) for i in range(GROUPS * Z)]
    return lax.ppermute(array, "dp", pairs)


def exchange(chunks, groups):
    return lax.all_to_all(
        chunks, "dp", split_axis=0, concat_axis=0, tiled=True, axis_index_groups=groups
    )


def take_last_kernel(len_ref, hidden_ref, out_ref, tile_ref, sem):
    seq_count, depth, width = tile_ref.shape
    spots = [len_ref[seq // 2, seq % 2] - 1 for seq in range(seq_count)]
    copies = []
    for seq, spot in enumerate(spots):
        rows = pl.ds(pl.multiple_of(spot & -depth, depth), depth)
        copies.append(
            pltpu.make_async_copy(hidden_ref.at[seq, rows, :], tile_ref.at[seq], sem.at[seq])
        )
        copies[-1].start()
    row_at = lax.broadcasted_iota(jnp.int32, (depth, width), 0)
    seq_at = lax.broadcasted_iota(jnp.int32, (seq_count, width), 0)
    rows = jnp.zeros((seq_count, width), jnp.float32)
    for seq, spot in enumerate(spots):
        copies[seq].wait()
        tile = tile_ref[seq].astype(jnp.float32)
        row = jnp.sum(jnp.where(row_at == (spot & (depth - 1)), tile, 0.0), axis=0, keepdims=True)
        rows = jnp.where(seq_at == seq, row, rows)
    out_ref[...] = rows.astype(jnp.bfloat16)


def last_rows_kernel(at_ref, r0, r1, r2, r3, gain_ref, out_ref, raw_ref, row_ref):
    y_at, x_lo_at, tensor_at = at_ref[0], at_ref[1], at_ref[2]
    refs = [r0, r1, r2, r3]
    seq_count, width = r0.shape
    rows = width // (XLO * Z)
    squares = None
    for k, ref in enumerate(refs):
        x = ref[...].astype(jnp.float32)
        raw_ref[k] = x
        part = jnp.sum(x * x, axis=-1, keepdims=True)
        squares = part if squares is None else squares + part
    scale = lax.rsqrt(squares / (len(refs) * width) + EPS)
    row_ref[...] = jnp.zeros_like(row_ref)
    for step in range(Y):
        slice_at = (y_at + step) & (Y - 1)
        normed = raw_ref[slice_at ^ tensor_at] * scale * gain_ref[
            :, pl.ds(pl.multiple_of(slice_at * width, width), width)
        ]
        normed = normed.astype(jnp.bfloat16).astype(jnp.float32)
        halves = [normed[:, : Z * rows], normed[:, Z * rows :]]
        row, lane = (0, step * XLO * rows) if step < Y - 1 else (8, 0)
        for x in range(XLO):
            half = jnp.where(x_lo_at == x, halves[0], halves[1])
            for z in range(Z):
                at = lane + x * rows
                row_ref[z, row : row + seq_count, at : at + rows] = half[
                    :, z * rows : (z + 1) * rows
                ]
    out_ref[...] = row_ref[...].astype(jnp.bfloat16)


def query_kernel(rows_ref, w0, w1, w2, w3, out_ref, acc_ref):
    depth, _ = w0.shape
    rows = rows_ref[...].astype(jnp.float32)
    total = None
    for step, w_ref in enumerate([w0, w1, w2, w3]):
        row, lane = (0, step * depth) if step < Y - 1 else (8, 0)
        lhs = rows[:, row : row + 8, lane : lane + depth].reshape(Z * 8, depth)
        part = jnp.dot(
            lhs.astype(jnp.bfloat16), w_ref[:, HEAD_DIM:], preferred_element_type=jnp.float32
        )
        total = part if total is None else total + part
    high = total.astype(jnp.bfloat16).astype(jnp.float32)
    low = (total - high).astype(jnp.bfloat16).astype(jnp.float32)
    both = high + pltpu.roll(low, 4, 0)
    for head in range(both.shape[1] // HEAD_DIM):
        block = both[:, head * HEAD_DIM : (head + 1) * HEAD_DIM]
        acc_ref[:, head * 8 : (head + 1) * 8, :] = block.reshape(Z, 8, HEAD_DIM)
    out_ref[...] = acc_ref[...].astype(jnp.bfloat16)


def kv_attend_kernel(
    at_ref,
    len_ref,
    x0_ref,
    x1_ref,
    x2_ref,
    x3_ref,
    own_ref,
    up_ref,
    down_ref,
    far_low_ref,
    far_high_ref,
    last_ref,
    gain_ref,
    qg_ref,
    kg_ref,
    out_ref,
    wk_ref,
    wv_ref,
    query_ref,
):
    x_refs = [x0_ref, x1_ref, x2_ref, x3_ref]
    _, slots, width = x0_ref.shape
    slices = len(x_refs)
    rows = width // (XLO * Z)
    seq = pl.program_id(0)
    heads = out_ref.shape[1]
    y_at, x_lo_at, tensor_at = at_ref[0], at_ref[1], at_ref[2]

    @pl.when(seq == 0)
    def _():
        low = Z // 2
        for step, parts in enumerate(
            [
                [own_ref.at[:low], own_ref.at[low:]],
                [up_ref.at[:low], up_ref.at[low:]],
                [far_low_ref, far_high_ref],
                [down_ref.at[:low], down_ref.at[low:]],
            ]
        ):
            base = ((y_at + step) & (Y - 1)) * width
            for x in range(XLO):
                half = base + (x_lo_at ^ x) * (Z * rows)
                for z in range(Z):
                    at = pl.ds(pl.multiple_of(half + z * rows, rows), rows)
                    block = slice(x * rows, (x + 1) * rows)
                    piece = parts[z // low].at[z % low]
                    wk_ref[at, :] = piece[block, : 2 * HEAD_DIM]
                    wv_ref[at, :HEAD_DIM] = piece[block, 2 * HEAD_DIM :]
                    start = (step * XLO + x) * rows
                    wv_ref[at, HEAD_DIM:] = last_ref[z, start : start + rows, :]
        parts = last_ref[:, Y * XLO * rows :, :].astype(jnp.float32)
        parts = jnp.sum(parts, axis=0)
        query_ref[...] = parts + pltpu.roll(parts, parts.shape[0] - 4, 0)

    squares = None
    for k in range(slices):
        x = x_refs[k][0].astype(jnp.float32)
        part = jnp.sum(x * x, axis=-1, keepdims=True)
        squares = part if squares is None else squares + part
    scale = lax.rsqrt(squares / (slices * width) + EPS)
    key_proj = value_proj = None
    for k in range(slices):
        x = x_refs[k][0].astype(jnp.float32)
        slice_at = tensor_at ^ k
        at = pl.ds(pl.multiple_of(slice_at * width, width), width)
        normed = (x * scale * gain_ref[:, at]).astype(jnp.bfloat16)
        kp = jnp.dot(normed, wk_ref[at, :], preferred_element_type=jnp.float32)
        vp = jnp.dot(normed, wv_ref[at, :], preferred_element_type=jnp.float32)
        key_proj = kp if key_proj is None else key_proj + kp
        value_proj = vp if value_proj is None else value_proj + vp
    query = query_ref[pl.ds(seq, heads, stride=8), :]
    query = (rms_rows(query) * qg_ref[...]).astype(jnp.bfloat16)
    first = lax.broadcasted_iota(jnp.int32, (heads, 1), 0) < heads // 2
    scores = []
    for h in range(2):
        key = key_proj[:, h * HEAD_DIM : (h + 1) * HEAD_DIM]
        key = (rms_rows(key) * kg_ref[...]).astype(jnp.bfloat16)
        scores.append(
            lax.dot_general(
                query, key, (((1,), (1,)), ((), ())), preferred_element_type=jnp.float32
            )
        )
    scores = jnp.where(first, scores[0], scores[1]) / math.sqrt(HEAD_DIM)
    positions = lax.broadcasted_iota(jnp.int32, (1, slots), 1)
    scores = jnp.where(positions < len_ref[seq >> 1, seq & 1], scores, -1e30)
    expo = jnp.exp(scores - jnp.max(scores, axis=-1, keepdims=True))
    weights = (expo / jnp.sum(expo, axis=-1, keepdims=True)).astype(jnp.bfloat16)
    value = value_proj.astype(jnp.bfloat16)
    mixed = jnp.dot(weights, value, preferred_element_type=jnp.float32)
    out_ref[0] = jnp.where(first, mixed[:, :HEAD_DIM], mixed[:, HEAD_DIM:])


SMEM = pl.BlockSpec(memory_space=pltpu.SMEM)
VMEM = pl.BlockSpec(memory_space=pltpu.VMEM)


def take_last_call(lengths, own):
    seq_count, _, width = own.shape
    return pl.pallas_call(
        take_last_kernel,
        in_specs=[SMEM, pl.BlockSpec(memory_space=pl.ANY)],
        out_specs=VMEM,
        out_shape=jax.ShapeDtypeStruct((seq_count, width), own.dtype),
        scratch_shapes=[
            pltpu.VMEM((seq_count, 16, width), own.dtype),
            pltpu.SemaphoreType.DMA((seq_count,)),
        ],
    )(lengths, own)


def last_rows_call(at, raw, gains):
    seq_count, width = raw[0].shape
    shape = (Z, 16, (Y - 1) * XLO * (width // (XLO * Z)))
    return pl.pallas_call(
        last_rows_kernel,
        in_specs=[SMEM] + [VMEM] * (len(raw) + 1),
        out_specs=VMEM,
        out_shape=jax.ShapeDtypeStruct(shape, jnp.bfloat16),
        scratch_shapes=[
            pltpu.VMEM((len(raw), seq_count, width), jnp.float32),
            pltpu.VMEM(shape, jnp.float32),
        ],
    )(at, *raw, gains)


def query_call(z_all, rest):
    shape = (Z, (rest[0].shape[1] // HEAD_DIM - 1) * 8, HEAD_DIM)
    tail = z_all.shape[1] // 16 - 1
    return pl.pallas_call(
        query_kernel,
        grid=(1,),
        in_specs=[pl.BlockSpec((Z, 16, z_all.shape[2]), lambda i: (0, tail, 0))]
        + [VMEM] * len(rest),
        out_specs=VMEM,
        out_shape=jax.ShapeDtypeStruct(shape, jnp.bfloat16),
        scratch_shapes=[pltpu.VMEM(shape, jnp.float32)],
    )(z_all, *rest)


def kv_attend(at, lengths, slices, pieces, last, gains, heads, qg, kg):
    seq_count, slots, width = slices[0].shape
    model_width = gains.size
    kv_width = 2 * HEAD_DIM
    x_spec = pl.BlockSpec((1, slots, width), lambda seq: (seq, 0, 0))
    return pl.pallas_call(
        kv_attend_kernel,
        grid=(seq_count,),
        in_specs=[SMEM, SMEM] + [x_spec] * len(slices) + [VMEM] * (len(pieces) + 4),
        out_specs=pl.BlockSpec((1, heads, HEAD_DIM), lambda seq: (seq, 0, 0)),
        out_shape=jax.ShapeDtypeStruct((seq_count, heads, HEAD_DIM), jnp.float32),
        scratch_shapes=[pltpu.VMEM((model_width, kv_width), jnp.bfloat16)] * 2
        + [pltpu.VMEM((heads * 8, HEAD_DIM), jnp.float32)],
        compiler_params=pltpu.CompilerParams(vmem_limit_bytes=40 * 1024 * 1024),
        cost_estimate=pl.CostEstimate(
            flops=4 * seq_count * slots * model_width * kv_width,
            bytes_accessed=2 * seq_count * slots * model_width + 4 * model_width * kv_width,
            transcendentals=seq_count * heads * slots,
        ),
    )(at, lengths, *slices, *pieces, last, gains, qg, kg)


def body(
    hidden, lengths, norm_gain, q_norm_gain, k_norm_gain, query_weight, key_weight, value_weight
):
    tensor_size = lax.axis_size("tensor")
    tensor_at = lax.axis_index("tensor")
    dp_at = lax.axis_index("dp")
    x_lo_at = (dp_at >> (Z.bit_length() - 1)) & (XLO - 1)
    y_at = dp_at >> ((Z * XLO).bit_length() - 1)
    at = jnp.stack([y_at, x_lo_at, tensor_at]).astype(jnp.int32)

    pair_count, _, seq_slots, width_local = hidden.shape
    seq_count = 2 * pair_count
    own = hidden.reshape(seq_count, seq_slots, width_local)
    rows_local, kv_width = key_weight.shape
    query_width = query_weight.shape[1]
    gains = norm_gain[None]

    kv_weight = jnp.concatenate([key_weight, value_weight], axis=1)
    kv_both = jnp.concatenate([kv_weight, swap_x_lo(kv_weight)])
    query_other = swap_x_lo(query_weight)
    last_own = take_last_call(lengths, own)
    last_raw = [last_own] + [swap_tensor(last_own, k) for k in range(1, tensor_size)]

    sent_own = lax.optimization_barrier((own, kv_both, query_other, *last_raw))[0]
    far = swap_tensor(sent_own, 2)
    peer = swap_tensor(sent_own, 1)

    block = kv_both[:, : kv_width + HEAD_DIM]
    rows = last_rows_call(at, last_raw, gains)
    z_all = exchange(
        jnp.concatenate([jnp.broadcast_to(block[None], (Z,) + block.shape), rows], axis=1),
        Z_GROUPS,
    )
    z_own = z_all[:, : block.shape[0]]
    z_up = shift(z_own, dy=-1)
    z_down = shift(z_own, dy=1)
    far_low = shift(z_up[: Z // 2], dy=-1)
    far_high = shift(z_down[Z // 2 :], dy=1)
    pieces = [z_own, z_up, z_down, far_low, far_high]

    rest = jnp.concatenate(
        [kv_both[:, kv_width + HEAD_DIM :], jnp.concatenate([query_weight, query_other])], axis=1
    )
    rest = [rest] + [shift(rest, dy=-step) for step in range(1, Y)]
    partial_q = query_call(z_all, rest)
    head = jnp.concatenate([array[:, :HEAD_DIM] for array in rest])
    last = exchange(
        jnp.concatenate([jnp.broadcast_to(head[None], (Z,) + head.shape), partial_q], axis=1),
        Z_GROUPS,
    )
    far_peer = swap_tensor(lax.optimization_barrier((far, last, *pieces))[0], 1)

    mixed = kv_attend(
        at,
        lengths,
        [own, peer, far, far_peer],
        pieces,
        last,
        gains,
        query_width // HEAD_DIM,
        q_norm_gain[None],
        k_norm_gain[None],
    ).reshape(seq_count, width_local)

    sent = mixed.astype(jnp.bfloat16)
    every = exchange(jnp.broadcast_to(sent[None], (GROUPS * Z,) + sent.shape), None)
    every = every.reshape(-1, 2, width_local)
    dots = jnp.dot(every[:, 0], every[:, 1].T, preferred_element_type=jnp.float32)
    every_f32 = every.astype(jnp.float32)
    norms = jnp.sum(every_f32 * every_f32, axis=-1).T
    part = jnp.concatenate([dots, norms], axis=0)
    parts = [part] + [swap_tensor(part, k) for k in range(1, tensor_size)]
    total = (parts[0] + parts[1]) + (parts[2] + parts[3])
    pairs = dots.shape[0]
    scales = lax.rsqrt(total[pairs:] + EPS)
    sim = SCORE_SCALE * total[:pairs] * scales[0][:, None] * scales[1][None, :]
    row_lse = jax.nn.logsumexp(sim, axis=1)
    col_lse = jax.nn.logsumexp(sim, axis=0)
    positive = jnp.sum(jnp.where(jnp.eye(pairs, dtype=bool), sim, 0.0), axis=0)
    all_loss = 0.5 * (row_lse + col_lse) - positive
    loss = jnp.mean(all_loss)
    pair_loss = lax.dynamic_slice_in_dim(all_loss, dp_at * pair_count, pair_count)
    own_scale = lax.dynamic_slice_in_dim(scales, dp_at * pair_count, pair_count, axis=1)
    embeddings = (mixed.reshape(pair_count, 2, width_local) * own_scale.T[:, :, None]).astype(
        jnp.bfloat16
    )
    return (embeddings, pair_loss, loss)


def solution(mesh):
    in_specs = (
        P("dp", None, None, "tensor"),
        P("dp", None),
        P(),
        P(),
        P(),
        P("dp", "tensor"),
        P("dp", "tensor"),
        P("dp", "tensor"),
    )
    out_specs = (P("dp", None, "tensor"), P("dp"), P())
    return jax.shard_map(body, mesh=mesh, in_specs=in_specs, out_specs=out_specs, check_vma=False)
```

```python
import math

import jax
import jax.numpy as jnp
from jax import lax
from jax.experimental import pallas as pl
from jax.experimental.pallas import tpu as pltpu
from jax.sharding import PartitionSpec as P

HEAD_DIM = 128
EPS = 1e-06
SCORE_SCALE = 20.0

Y, XLO, Z = 4, 2, 8
XHI, CORES = 2, 2
GROUPS = Y * XLO
Z_GROUPS = [[g * Z + z for z in range(Z)] for g in range(GROUPS)]


def rms_rows(values):
    return values * lax.rsqrt(jnp.mean(values * values, axis=-1, keepdims=True) + EPS)


def shift(array, dx=0, dy=0, dz=0):
    pairs = []
    for y in range(Y):
        for x in range(XHI * XLO):
            for z in range(Z):
                for core in range(CORES):

                    def at(x, y, z):
                        x_hi, x_lo = divmod(x, XLO)
                        dp = (y * XLO + x_lo) * Z + z
                        return dp * (XHI * CORES) + x_hi * CORES + core

                    there = at((x + dx) % (XHI * XLO), (y + dy) % Y, (z + dz) % Z)
                    pairs.append((at(x, y, z), there))
    return lax.ppermute(array, ("dp", "tensor"), pairs)


def swap_tensor(array, mask):
    size = XHI * CORES
    return lax.ppermute(array, "tensor", [(i, i ^ mask) for i in range(size)])


def swap_x_lo(array):
    pairs = [(i, (i // Z ^ 1) * Z + i % Z) for i in range(GROUPS * Z)]
    return lax.ppermute(array, "dp", pairs)


def exchange(chunks, groups):
    return lax.all_to_all(
        chunks, "dp", split_axis=0, concat_axis=0, tiled=True, axis_index_groups=groups
    )


def take_last_kernel(len_ref, hidden_ref, out_ref, tile_ref, sem):
    seq_count, depth, width = tile_ref.shape
    spots = [len_ref[seq // 2, seq % 2] - 1 for seq in range(seq_count)]
    copies = []
    for seq, spot in enumerate(spots):
        rows = pl.ds(pl.multiple_of(spot & -depth, depth), depth)
        copies.append(
            pltpu.make_async_copy(hidden_ref.at[seq, rows, :], tile_ref.at[seq], sem.at[seq])
        )
        copies[-1].start()
    row_at = lax.broadcasted_iota(jnp.int32, (depth, width), 0)
    seq_at = lax.broadcasted_iota(jnp.int32, (seq_count, width), 0)
    rows = jnp.zeros((seq_count, width), jnp.float32)
    for seq, spot in enumerate(spots):
        copies[seq].wait()
        tile = tile_ref[seq].astype(jnp.float32)
        row = jnp.sum(jnp.where(row_at == (spot & (depth - 1)), tile, 0.0), axis=0, keepdims=True)
        rows = jnp.where(seq_at == seq, row, rows)
    out_ref[...] = rows.astype(jnp.bfloat16)


def last_rows_kernel(at_ref, r0, r1, r2, r3, gain_ref, out_ref, raw_ref, row_ref):
    y_at, x_lo_at, tensor_at = at_ref[0], at_ref[1], at_ref[2]
    refs = [r0, r1, r2, r3]
    seq_count, width = r0.shape
    rows = width // (XLO * Z)
    squares = None
    for k, ref in enumerate(refs):
        x = ref[...].astype(jnp.float32)
        raw_ref[k] = x
        part = jnp.sum(x * x, axis=-1, keepdims=True)
        squares = part if squares is None else squares + part
    scale = lax.rsqrt(squares / (len(refs) * width) + EPS)
    row_ref[...] = jnp.zeros_like(row_ref)
    for step in range(Y):
        slice_at = (y_at + step) & (Y - 1)
        normed = raw_ref[slice_at ^ tensor_at] * scale * gain_ref[
            :, pl.ds(pl.multiple_of(slice_at * width, width), width)
        ]
        normed = normed.astype(jnp.bfloat16).astype(jnp.float32)
        halves = [normed[:, : Z * rows], normed[:, Z * rows :]]
        row, lane = (0, step * XLO * rows) if step < Y - 1 else (8, 0)
        for x in range(XLO):
            half = jnp.where(x_lo_at == x, halves[0], halves[1])
            for z in range(Z):
                at = lane + x * rows
                row_ref[z, row : row + seq_count, at : at + rows] = half[
                    :, z * rows : (z + 1) * rows
                ]
    out_ref[...] = row_ref[...].astype(jnp.bfloat16)


def query_kernel(rows_ref, w0, w1, w2, w3, out_ref, acc_ref):
    depth, _ = w0.shape
    rows = rows_ref[...].astype(jnp.float32)
    total = None
    for step, w_ref in enumerate([w0, w1, w2, w3]):
        row, lane = (0, step * depth) if step < Y - 1 else (8, 0)
        lhs = rows[:, row : row + 8, lane : lane + depth].reshape(Z * 8, depth)
        part = jnp.dot(
            lhs.astype(jnp.bfloat16), w_ref[:, HEAD_DIM:], preferred_element_type=jnp.float32
        )
        total = part if total is None else total + part
    high = total.astype(jnp.bfloat16).astype(jnp.float32)
    low = (total - high).astype(jnp.bfloat16).astype(jnp.float32)
    both = high + pltpu.roll(low, 4, 0)
    for head in range(both.shape[1] // HEAD_DIM):
        block = both[:, head * HEAD_DIM : (head + 1) * HEAD_DIM]
        acc_ref[:, head * 8 : (head + 1) * 8, :] = block.reshape(Z, 8, HEAD_DIM)
    out_ref[...] = acc_ref[...].astype(jnp.bfloat16)


def kv_attend_kernel(
    at_ref,
    len_ref,
    x0_ref,
    x1_ref,
    x2_ref,
    x3_ref,
    own_ref,
    up_ref,
    down_ref,
    far_low_ref,
    far_high_ref,
    last_ref,
    gain_ref,
    qg_ref,
    kg_ref,
    out_ref,
    wk_ref,
    wv_ref,
    parts_ref,
    query_ref,
    sem,
):
    x_refs = [x0_ref, x1_ref, x2_ref, x3_ref]
    _, slots, width = x0_ref.shape
    slices = len(x_refs)
    rows = width // (XLO * Z)
    seq = pl.program_id(0)
    heads = out_ref.shape[1]
    y_at, x_lo_at, tensor_at = at_ref[0], at_ref[1], at_ref[2]

    @pl.when(seq == 0)
    def _():
        low = Z // 2
        copies = []

        def start(source, target):
            copy = pltpu.make_async_copy(source, target, sem.at[len(copies)])
            copy.start()
            copies.append(copy)

        tail = pl.ds(Y * XLO * rows, parts_ref.shape[1])
        start(last_ref.at[:, tail, :], parts_ref)
        for step, halves in enumerate(
            [[own_ref], [up_ref], [far_low_ref, far_high_ref], [down_ref]]
        ):
            y = (y_at + step) & (Y - 1)
            for x in range(XLO):
                block = pl.ds(x * rows, rows)
                for half, piece in enumerate(halves):
                    zs = pl.ds(half * low, piece.shape[0])
                    wk_at = wk_ref.at[y, x_lo_at ^ x, zs]
                    start(piece.at[:, block, pl.ds(0, 2 * HEAD_DIM)], wk_at)
                    wv_at = wv_ref.at[y, x_lo_at ^ x, zs, :, pl.ds(0, HEAD_DIM)]
                    start(piece.at[:, block, pl.ds(2 * HEAD_DIM, HEAD_DIM)], wv_at)
                block = pl.ds((step * XLO + x) * rows, rows)
                wv_at = wv_ref.at[y, x_lo_at ^ x, :, :, pl.ds(HEAD_DIM, HEAD_DIM)]
                start(last_ref.at[:, block, :], wv_at)
        for copy in copies:
            copy.wait()
        parts = jnp.sum(parts_ref[...].astype(jnp.float32), axis=0)
        query_ref[...] = parts + pltpu.roll(parts, parts.shape[0] - 4, 0)

    squares = None
    for k in range(slices):
        x = x_refs[k][0].astype(jnp.float32)
        part = jnp.sum(x * x, axis=-1, keepdims=True)
        squares = part if squares is None else squares + part
    scale = lax.rsqrt(squares / (slices * width) + EPS)
    key_proj = value_proj = None
    for k in range(slices):
        x = x_refs[k][0].astype(jnp.float32)
        slice_at = tensor_at ^ k
        at = pl.ds(pl.multiple_of(slice_at * width, width), width)
        normed = (x * scale * gain_ref[:, at]).astype(jnp.bfloat16)
        wk = wk_ref[slice_at].reshape(width, -1)
        wv = wv_ref[slice_at].reshape(width, -1)
        kp = jnp.dot(normed, wk, preferred_element_type=jnp.float32)
        vp = jnp.dot(normed, wv, preferred_element_type=jnp.float32)
        key_proj = kp if key_proj is None else key_proj + kp
        value_proj = vp if value_proj is None else value_proj + vp
    query = query_ref[pl.ds(seq, heads, stride=8), :]
    query = (rms_rows(query) * qg_ref[...]).astype(jnp.bfloat16)
    first = lax.broadcasted_iota(jnp.int32, (heads, 1), 0) < heads // 2
    scores = []
    for h in range(2):
        key = key_proj[:, h * HEAD_DIM : (h + 1) * HEAD_DIM]
        key = (rms_rows(key) * kg_ref[...]).astype(jnp.bfloat16)
        scores.append(
            lax.dot_general(
                query, key, (((1,), (1,)), ((), ())), preferred_element_type=jnp.float32
            )
        )
    scores = jnp.where(first, scores[0], scores[1]) / math.sqrt(HEAD_DIM)
    positions = lax.broadcasted_iota(jnp.int32, (1, slots), 1)
    scores = jnp.where(positions < len_ref[seq >> 1, seq & 1], scores, -1e30)
    expo = jnp.exp(scores - jnp.max(scores, axis=-1, keepdims=True))
    weights = (expo / jnp.sum(expo, axis=-1, keepdims=True)).astype(jnp.bfloat16)
    value = value_proj.astype(jnp.bfloat16)
    mixed = jnp.dot(weights, value, preferred_element_type=jnp.float32)
    out_ref[0] = jnp.where(first, mixed[:, :HEAD_DIM], mixed[:, HEAD_DIM:])


SMEM = pl.BlockSpec(memory_space=pltpu.SMEM)
VMEM = pl.BlockSpec(memory_space=pltpu.VMEM)


def take_last_call(lengths, own):
    seq_count, _, width = own.shape
    return pl.pallas_call(
        take_last_kernel,
        in_specs=[SMEM, pl.BlockSpec(memory_space=pl.ANY)],
        out_specs=VMEM,
        out_shape=jax.ShapeDtypeStruct((seq_count, width), own.dtype),
        scratch_shapes=[
            pltpu.VMEM((seq_count, 16, width), own.dtype),
            pltpu.SemaphoreType.DMA((seq_count,)),
        ],
    )(lengths, own)


def last_rows_call(at, raw, gains):
    seq_count, width = raw[0].shape
    shape = (Z, 16, (Y - 1) * XLO * (width // (XLO * Z)))
    return pl.pallas_call(
        last_rows_kernel,
        in_specs=[SMEM] + [VMEM] * (len(raw) + 1),
        out_specs=VMEM,
        out_shape=jax.ShapeDtypeStruct(shape, jnp.bfloat16),
        scratch_shapes=[
            pltpu.VMEM((len(raw), seq_count, width), jnp.float32),
            pltpu.VMEM(shape, jnp.float32),
        ],
    )(at, *raw, gains)


def query_call(z_all, rest):
    shape = (Z, (rest[0].shape[1] // HEAD_DIM - 1) * 8, HEAD_DIM)
    tail = z_all.shape[1] // 16 - 1
    return pl.pallas_call(
        query_kernel,
        grid=(1,),
        in_specs=[pl.BlockSpec((Z, 16, z_all.shape[2]), lambda i: (0, tail, 0))]
        + [VMEM] * len(rest),
        out_specs=VMEM,
        out_shape=jax.ShapeDtypeStruct(shape, jnp.bfloat16),
        scratch_shapes=[pltpu.VMEM(shape, jnp.float32)],
    )(z_all, *rest)


def kv_attend(at, lengths, slices, pieces, last, gains, heads, qg, kg):
    seq_count, slots, width = slices[0].shape
    model_width = gains.size
    kv_width = 2 * HEAD_DIM
    rows = model_width // (Y * XLO * Z)
    x_spec = pl.BlockSpec((1, slots, width), lambda seq: (seq, 0, 0))
    return pl.pallas_call(
        kv_attend_kernel,
        grid=(seq_count,),
        in_specs=[SMEM, SMEM]
        + [x_spec] * len(slices)
        + [pl.BlockSpec(memory_space=pltpu.HBM)] * (len(pieces) + 1)
        + [VMEM] * 3,
        out_specs=pl.BlockSpec((1, heads, HEAD_DIM), lambda seq: (seq, 0, 0)),
        out_shape=jax.ShapeDtypeStruct((seq_count, heads, HEAD_DIM), jnp.float32),
        scratch_shapes=[pltpu.VMEM((Y, XLO, Z, rows, kv_width), jnp.bfloat16)] * 2
        + [
            pltpu.VMEM((Z, heads * 8, HEAD_DIM), jnp.bfloat16),
            pltpu.VMEM((heads * 8, HEAD_DIM), jnp.float32),
            pltpu.SemaphoreType.DMA((1 + XLO * (3 * Y + 2),)),
        ],
        compiler_params=pltpu.CompilerParams(vmem_limit_bytes=40 * 1024 * 1024),
        cost_estimate=pl.CostEstimate(
            flops=4 * seq_count * slots * model_width * kv_width,
            bytes_accessed=2 * seq_count * slots * model_width + 4 * model_width * kv_width,
            transcendentals=seq_count * heads * slots,
        ),
    )(at, lengths, *slices, *pieces, last, gains, qg, kg)


def body(
    hidden, lengths, norm_gain, q_norm_gain, k_norm_gain, query_weight, key_weight, value_weight
):
    tensor_size = lax.axis_size("tensor")
    tensor_at = lax.axis_index("tensor")
    dp_at = lax.axis_index("dp")
    x_lo_at = (dp_at >> (Z.bit_length() - 1)) & (XLO - 1)
    y_at = dp_at >> ((Z * XLO).bit_length() - 1)
    at = jnp.stack([y_at, x_lo_at, tensor_at]).astype(jnp.int32)

    pair_count, _, seq_slots, width_local = hidden.shape
    seq_count = 2 * pair_count
    own = hidden.reshape(seq_count, seq_slots, width_local)
    rows_local, kv_width = key_weight.shape
    query_width = query_weight.shape[1]
    gains = norm_gain[None]

    kv_weight = jnp.concatenate([key_weight, value_weight], axis=1)
    kv_both = jnp.concatenate([kv_weight, swap_x_lo(kv_weight)])
    query_other = swap_x_lo(query_weight)
    last_own = take_last_call(lengths, own)
    last_raw = [last_own] + [swap_tensor(last_own, k) for k in range(1, tensor_size)]

    sent_own = lax.optimization_barrier((own, kv_both, query_other, *last_raw))[0]
    far = swap_tensor(sent_own, 2)
    peer = swap_tensor(sent_own, 1)

    block = kv_both[:, : kv_width + HEAD_DIM]
    rows = last_rows_call(at, last_raw, gains)
    rows, _ = lax.optimization_barrier((rows, query_other))
    z_all = exchange(
        jnp.concatenate([jnp.broadcast_to(block[None], (Z,) + block.shape), rows], axis=1),
        Z_GROUPS,
    )

    rest = jnp.concatenate(
        [kv_both[:, kv_width + HEAD_DIM :], jnp.concatenate([query_weight, query_other])], axis=1
    )
    rest = [rest] + [shift(rest, dy=-step) for step in range(1, Y)]
    partial_q = query_call(z_all, rest)
    head = jnp.concatenate([array[:, :HEAD_DIM] for array in rest])

    z_own = lax.optimization_barrier((z_all[:, : block.shape[0]], *rest))[0]
    z_up = shift(z_own, dy=-1)
    z_down = shift(z_own, dy=1)
    far_low = shift(z_up[: Z // 2], dy=-1)
    far_high = shift(z_down[Z // 2 :], dy=1)
    pieces = [z_own, z_up, z_down, far_low, far_high]

    corner = swap_tensor(z_own[:, :16, :HEAD_DIM], 1)
    last = exchange(
        jnp.concatenate(
            [jnp.broadcast_to(head[None], (Z,) + head.shape), partial_q, corner], axis=1
        ),
        Z_GROUPS,
    )
    far_peer = swap_tensor(lax.optimization_barrier((far, z_up, z_down))[0], 1)

    mixed = kv_attend(
        at,
        lengths,
        [own, peer, far, far_peer],
        pieces,
        last,
        gains,
        query_width // HEAD_DIM,
        q_norm_gain[None],
        k_norm_gain[None],
    ).reshape(seq_count, width_local)

    sent = mixed.astype(jnp.bfloat16)
    every = exchange(jnp.broadcast_to(sent[None], (GROUPS * Z,) + sent.shape), None)
    every = every.reshape(-1, 2, width_local)
    dots = jnp.dot(every[:, 0], every[:, 1].T, preferred_element_type=jnp.float32)
    every_f32 = every.astype(jnp.float32)
    norms = jnp.sum(every_f32 * every_f32, axis=-1).T
    part = jnp.concatenate([dots, norms], axis=0)
    parts = [part] + [swap_tensor(part, k) for k in range(1, tensor_size)]
    total = (parts[0] + parts[1]) + (parts[2] + parts[3])
    pairs = dots.shape[0]
    scales = lax.rsqrt(total[pairs:] + EPS)
    sim = SCORE_SCALE * total[:pairs] * scales[0][:, None] * scales[1][None, :]
    row_lse = jax.nn.logsumexp(sim, axis=1)
    col_lse = jax.nn.logsumexp(sim, axis=0)
    positive = jnp.sum(jnp.where(jnp.eye(pairs, dtype=bool), sim, 0.0), axis=0)
    all_loss = 0.5 * (row_lse + col_lse) - positive
    loss = jnp.mean(all_loss)
    pair_loss = lax.dynamic_slice_in_dim(all_loss, dp_at * pair_count, pair_count)
    own_scale = lax.dynamic_slice_in_dim(scales, dp_at * pair_count, pair_count, axis=1)
    embeddings = (mixed.reshape(pair_count, 2, width_local) * own_scale.T[:, :, None]).astype(
        jnp.bfloat16
    )
    return (embeddings, pair_loss, loss)


def solution(mesh):
    in_specs = (
        P("dp", None, None, "tensor"),
        P("dp", None),
        P(),
        P(),
        P(),
        P("dp", "tensor"),
        P("dp", "tensor"),
        P("dp", "tensor"),
    )
    out_specs = (P("dp", None, "tensor"), P("dp"), P())
    return jax.shard_map(body, mesh=mesh, in_specs=in_specs, out_specs=out_specs, check_vma=False)
```

```python
import math

import jax
import jax.numpy as jnp
from jax import lax
from jax.experimental import pallas as pl
from jax.experimental.pallas import tpu as pltpu
from jax.sharding import PartitionSpec as P

HEAD_DIM = 128
EPS = 1e-06
SCORE_SCALE = 20.0

Y, XLO, Z = 4, 2, 8
XHI, CORES = 2, 2
GROUPS = Y * XLO
Z_GROUPS = [[g * Z + z for z in range(Z)] for g in range(GROUPS)]


def rms_rows(values):
    return values * lax.rsqrt(jnp.mean(values * values, axis=-1, keepdims=True) + EPS)


def shift(array, dx=0, dy=0, dz=0):
    pairs = []
    for y in range(Y):
        for x in range(XHI * XLO):
            for z in range(Z):
                for core in range(CORES):

                    def at(x, y, z):
                        x_hi, x_lo = divmod(x, XLO)
                        dp = (y * XLO + x_lo) * Z + z
                        return dp * (XHI * CORES) + x_hi * CORES + core

                    there = at((x + dx) % (XHI * XLO), (y + dy) % Y, (z + dz) % Z)
                    pairs.append((at(x, y, z), there))
    return lax.ppermute(array, ("dp", "tensor"), pairs)


def swap_tensor(array, mask):
    size = XHI * CORES
    return lax.ppermute(array, "tensor", [(i, i ^ mask) for i in range(size)])


def swap_x_lo(array):
    pairs = [(i, (i // Z ^ 1) * Z + i % Z) for i in range(GROUPS * Z)]
    return lax.ppermute(array, "dp", pairs)


def exchange(chunks, groups):
    return lax.all_to_all(
        chunks, "dp", split_axis=0, concat_axis=0, tiled=True, axis_index_groups=groups
    )


def take_last_kernel(len_ref, hidden_ref, out_ref, tile_ref, sem):
    seq_count, depth, width = tile_ref.shape
    spots = [len_ref[seq // 2, seq % 2] - 1 for seq in range(seq_count)]
    copies = []
    for seq, spot in enumerate(spots):
        rows = pl.ds(pl.multiple_of(spot & -depth, depth), depth)
        copies.append(
            pltpu.make_async_copy(hidden_ref.at[seq, rows, :], tile_ref.at[seq], sem.at[seq])
        )
        copies[-1].start()
    row_at = lax.broadcasted_iota(jnp.int32, (depth, width), 0)
    seq_at = lax.broadcasted_iota(jnp.int32, (seq_count, width), 0)
    rows = jnp.zeros((seq_count, width), jnp.float32)
    for seq, spot in enumerate(spots):
        copies[seq].wait()
        tile = tile_ref[seq].astype(jnp.float32)
        row = jnp.sum(jnp.where(row_at == (spot & (depth - 1)), tile, 0.0), axis=0, keepdims=True)
        rows = jnp.where(seq_at == seq, row, rows)
    out_ref[...] = rows.astype(jnp.bfloat16)


def last_rows_kernel(at_ref, r0, r1, r2, r3, gain_ref, out_ref, raw_ref, row_ref):
    y_at, x_lo_at, tensor_at = at_ref[0], at_ref[1], at_ref[2]
    refs = [r0, r1, r2, r3]
    seq_count, width = r0.shape
    rows = width // (XLO * Z)
    squares = None
    for k, ref in enumerate(refs):
        x = ref[...].astype(jnp.float32)
        raw_ref[k] = x
        part = jnp.sum(x * x, axis=-1, keepdims=True)
        squares = part if squares is None else squares + part
    scale = lax.rsqrt(squares / (len(refs) * width) + EPS)
    row_ref[...] = jnp.zeros_like(row_ref)
    for step in range(Y):
        slice_at = (y_at + step) & (Y - 1)
        normed = raw_ref[slice_at ^ tensor_at] * scale * gain_ref[
            :, pl.ds(pl.multiple_of(slice_at * width, width), width)
        ]
        normed = normed.astype(jnp.bfloat16).astype(jnp.float32)
        halves = [normed[:, : Z * rows], normed[:, Z * rows :]]
        row, lane = (0, step * XLO * rows) if step < Y - 1 else (8, 0)
        for x in range(XLO):
            half = jnp.where(x_lo_at == x, halves[0], halves[1])
            for z in range(Z):
                at = lane + x * rows
                row_ref[z, row : row + seq_count, at : at + rows] = half[
                    :, z * rows : (z + 1) * rows
                ]
    out_ref[...] = row_ref[...].astype(jnp.bfloat16)


def query_kernel(rows_ref, w0, w1, w2, w3, out_ref, acc_ref):
    depth, _ = w0.shape
    rows = rows_ref[...].astype(jnp.float32)
    total = None
    for step, w_ref in enumerate([w0, w1, w2, w3]):
        row, lane = (0, step * depth) if step < Y - 1 else (8, 0)
        lhs = rows[:, row : row + 8, lane : lane + depth].reshape(Z * 8, depth)
        part = jnp.dot(
            lhs.astype(jnp.bfloat16), w_ref[:, HEAD_DIM:], preferred_element_type=jnp.float32
        )
        total = part if total is None else total + part
    high = total.astype(jnp.bfloat16).astype(jnp.float32)
    low = (total - high).astype(jnp.bfloat16).astype(jnp.float32)
    both = high + pltpu.roll(low, 4, 0)
    for head in range(both.shape[1] // HEAD_DIM):
        block = both[:, head * HEAD_DIM : (head + 1) * HEAD_DIM]
        acc_ref[:, head * 8 : (head + 1) * 8, :] = block.reshape(Z, 8, HEAD_DIM)
    out_ref[...] = acc_ref[...].astype(jnp.bfloat16)


def kv_attend_kernel(
    at_ref,
    len_ref,
    x0_ref,
    x1_ref,
    x2_ref,
    x3_ref,
    own_ref,
    up_ref,
    down_ref,
    far_low_ref,
    far_high_ref,
    last_ref,
    part_q_ref,
    gain_ref,
    qg_ref,
    kg_ref,
    out_ref,
    wk_ref,
    wv_ref,
    query_ref,
    sem,
):
    x_refs = [x0_ref, x1_ref, x2_ref, x3_ref]
    _, slots, width = x0_ref.shape
    slices = len(x_refs)
    rows = width // (XLO * Z)
    seq = pl.program_id(0)
    heads = out_ref.shape[1]
    y_at, x_lo_at, tensor_at = at_ref[0], at_ref[1], at_ref[2]

    @pl.when(seq == 0)
    def _():
        low = Z // 2
        copies = []

        def start(source, target):
            copy = pltpu.make_async_copy(source, target, sem.at[len(copies)])
            copy.start()
            copies.append(copy)

        for step, halves in enumerate(
            [[own_ref], [up_ref], [far_low_ref, far_high_ref], [down_ref]]
        ):
            y = (y_at + step) & (Y - 1)
            for x in range(XLO):
                block = pl.ds(x * rows, rows)
                for half, piece in enumerate(halves):
                    zs = pl.ds(half * low, piece.shape[0])
                    wk_at = wk_ref.at[y, x_lo_at ^ x, zs]
                    start(piece.at[:, block, pl.ds(0, 2 * HEAD_DIM)], wk_at)
                    wv_at = wv_ref.at[y, x_lo_at ^ x, zs, :, pl.ds(0, HEAD_DIM)]
                    start(piece.at[:, block, pl.ds(2 * HEAD_DIM, HEAD_DIM)], wv_at)
                block = pl.ds((step * XLO + x) * rows, rows)
                wv_at = wv_ref.at[y, x_lo_at ^ x, :, :, pl.ds(HEAD_DIM, HEAD_DIM)]
                start(last_ref.at[:, block, :], wv_at)
        for copy in copies:
            copy.wait()
        parts = jnp.sum(part_q_ref[...].astype(jnp.float32), axis=0)
        query_ref[...] = parts + pltpu.roll(parts, parts.shape[0] - 4, 0)

    squares = None
    for k in range(slices):
        x = x_refs[k][0].astype(jnp.float32)
        part = jnp.sum(x * x, axis=-1, keepdims=True)
        squares = part if squares is None else squares + part
    scale = lax.rsqrt(squares / (slices * width) + EPS)
    key_proj = value_proj = None
    for k in range(slices):
        x = x_refs[k][0].astype(jnp.float32)
        slice_at = tensor_at ^ k
        at = pl.ds(pl.multiple_of(slice_at * width, width), width)
        normed = (x * scale * gain_ref[:, at]).astype(jnp.bfloat16)
        wk = wk_ref[slice_at].reshape(width, -1)
        wv = wv_ref[slice_at].reshape(width, -1)
        kp = jnp.dot(normed, wk, preferred_element_type=jnp.float32)
        vp = jnp.dot(normed, wv, preferred_element_type=jnp.float32)
        key_proj = kp if key_proj is None else key_proj + kp
        value_proj = vp if value_proj is None else value_proj + vp
    query = query_ref[pl.ds(seq, heads, stride=8), :]
    query = (rms_rows(query) * qg_ref[...]).astype(jnp.bfloat16)
    first = lax.broadcasted_iota(jnp.int32, (heads, 1), 0) < heads // 2
    scores = []
    for h in range(2):
        key = key_proj[:, h * HEAD_DIM : (h + 1) * HEAD_DIM]
        key = (rms_rows(key) * kg_ref[...]).astype(jnp.bfloat16)
        scores.append(
            lax.dot_general(
                query, key, (((1,), (1,)), ((), ())), preferred_element_type=jnp.float32
            )
        )
    scores = jnp.where(first, scores[0], scores[1]) / math.sqrt(HEAD_DIM)
    positions = lax.broadcasted_iota(jnp.int32, (1, slots), 1)
    scores = jnp.where(positions < len_ref[seq >> 1, seq & 1], scores, -1e30)
    expo = jnp.exp(scores - jnp.max(scores, axis=-1, keepdims=True))
    weights = (expo / jnp.sum(expo, axis=-1, keepdims=True)).astype(jnp.bfloat16)
    value = value_proj.astype(jnp.bfloat16)
    mixed = jnp.dot(weights, value, preferred_element_type=jnp.float32)
    out_ref[0] = jnp.where(first, mixed[:, :HEAD_DIM], mixed[:, HEAD_DIM:])


SMEM = pl.BlockSpec(memory_space=pltpu.SMEM)
VMEM = pl.BlockSpec(memory_space=pltpu.VMEM)


def take_last_call(lengths, own):
    seq_count, _, width = own.shape
    return pl.pallas_call(
        take_last_kernel,
        in_specs=[SMEM, pl.BlockSpec(memory_space=pl.ANY)],
        out_specs=VMEM,
        out_shape=jax.ShapeDtypeStruct((seq_count, width), own.dtype),
        scratch_shapes=[
            pltpu.VMEM((seq_count, 16, width), own.dtype),
            pltpu.SemaphoreType.DMA((seq_count,)),
        ],
    )(lengths, own)


def last_rows_call(at, raw, gains):
    seq_count, width = raw[0].shape
    shape = (Z, 16, (Y - 1) * XLO * (width // (XLO * Z)))
    return pl.pallas_call(
        last_rows_kernel,
        in_specs=[SMEM] + [VMEM] * (len(raw) + 1),
        out_specs=VMEM,
        out_shape=jax.ShapeDtypeStruct(shape, jnp.bfloat16),
        scratch_shapes=[
            pltpu.VMEM((len(raw), seq_count, width), jnp.float32),
            pltpu.VMEM(shape, jnp.float32),
        ],
    )(at, *raw, gains)


def query_call(z_all, rest):
    shape = (Z, (rest[0].shape[1] // HEAD_DIM - 1) * 8, HEAD_DIM)
    tail = z_all.shape[1] // 16 - 1
    return pl.pallas_call(
        query_kernel,
        grid=(1,),
        in_specs=[pl.BlockSpec((Z, 16, z_all.shape[2]), lambda i: (0, tail, 0))]
        + [VMEM] * len(rest),
        out_specs=VMEM,
        out_shape=jax.ShapeDtypeStruct(shape, jnp.bfloat16),
        scratch_shapes=[pltpu.VMEM(shape, jnp.float32)],
    )(z_all, *rest)


def kv_attend(at, lengths, slices, pieces, last, partial_q, gains, qg, kg):
    seq_count, slots, width = slices[0].shape
    model_width = gains.size
    heads = partial_q.shape[1] // 8
    kv_width = 2 * HEAD_DIM
    rows = model_width // (Y * XLO * Z)
    x_spec = pl.BlockSpec((1, slots, width), lambda seq: (seq, 0, 0))
    return pl.pallas_call(
        kv_attend_kernel,
        grid=(seq_count,),
        in_specs=[SMEM, SMEM]
        + [x_spec] * len(slices)
        + [pl.BlockSpec(memory_space=pltpu.HBM)] * (len(pieces) + 1)
        + [VMEM] * 4,
        out_specs=pl.BlockSpec((1, heads, HEAD_DIM), lambda seq: (seq, 0, 0)),
        out_shape=jax.ShapeDtypeStruct((seq_count, heads, HEAD_DIM), jnp.float32),
        scratch_shapes=[pltpu.VMEM((Y, XLO, Z, rows, kv_width), jnp.bfloat16)] * 2
        + [
            pltpu.VMEM((heads * 8, HEAD_DIM), jnp.float32),
            pltpu.SemaphoreType.DMA((XLO * (3 * Y + 2),)),
        ],
        compiler_params=pltpu.CompilerParams(vmem_limit_bytes=58 * 1024 * 1024),
        cost_estimate=pl.CostEstimate(
            flops=4 * seq_count * slots * model_width * kv_width,
            bytes_accessed=2 * seq_count * slots * model_width + 4 * model_width * kv_width,
            transcendentals=seq_count * heads * slots,
        ),
    )(at, lengths, *slices, *pieces, last, partial_q, gains, qg, kg)


def body(
    hidden, lengths, norm_gain, q_norm_gain, k_norm_gain, query_weight, key_weight, value_weight
):
    tensor_size = lax.axis_size("tensor")
    tensor_at = lax.axis_index("tensor")
    dp_at = lax.axis_index("dp")
    x_lo_at = (dp_at >> (Z.bit_length() - 1)) & (XLO - 1)
    y_at = dp_at >> ((Z * XLO).bit_length() - 1)
    at = jnp.stack([y_at, x_lo_at, tensor_at]).astype(jnp.int32)

    pair_count, _, seq_slots, width_local = hidden.shape
    seq_count = 2 * pair_count
    own = hidden.reshape(seq_count, seq_slots, width_local)
    rows_local, kv_width = key_weight.shape
    gains = norm_gain[None]

    kv_weight = jnp.concatenate([key_weight, value_weight], axis=1)
    kv_both = jnp.concatenate([kv_weight, swap_x_lo(kv_weight)])
    query_other = swap_x_lo(query_weight)
    last_own = take_last_call(lengths, own)
    last_raw = [last_own] + [swap_tensor(last_own, k) for k in range(1, tensor_size)]

    sent_own = lax.optimization_barrier((own, kv_both, query_other, *last_raw))[0]
    far = swap_tensor(sent_own, 2)
    peer = swap_tensor(sent_own, 1)

    block = kv_both[:, : kv_width + HEAD_DIM]
    rows = last_rows_call(at, last_raw, gains)
    rows, _ = lax.optimization_barrier((rows, query_other))
    z_all = exchange(
        jnp.concatenate([jnp.broadcast_to(block[None], (Z,) + block.shape), rows], axis=1),
        Z_GROUPS,
    )

    rest = jnp.concatenate(
        [kv_both[:, kv_width + HEAD_DIM :], jnp.concatenate([query_weight, query_other])], axis=1
    )
    rest = [rest] + [shift(rest, dy=-step) for step in range(1, Y)]
    partial_q = query_call(z_all, rest)
    head = jnp.concatenate([array[:, :HEAD_DIM] for array in rest])

    z_own = lax.optimization_barrier((z_all[:, : block.shape[0]], *rest))[0]
    z_up = shift(z_own, dy=-1)
    z_down = shift(z_own, dy=1)
    far_low = shift(z_up[: Z // 2], dy=-1)
    far_high = shift(z_down[Z // 2 :], dy=1)
    pieces = [z_own, z_up, z_down, far_low, far_high]

    last = exchange(jnp.broadcast_to(head[None], (Z,) + head.shape), Z_GROUPS)
    partial_q = exchange(lax.optimization_barrier((partial_q, last))[0], Z_GROUPS)
    far_peer = swap_tensor(lax.optimization_barrier((far, z_up, z_down, last))[0], 1)

    mixed = kv_attend(
        at,
        lengths,
        [own, peer, far, far_peer],
        pieces,
        last,
        partial_q,
        gains,
        q_norm_gain[None],
        k_norm_gain[None],
    ).reshape(seq_count, width_local)

    sent = mixed.astype(jnp.bfloat16)
    every = exchange(jnp.broadcast_to(sent[None], (GROUPS * Z,) + sent.shape), None)
    every = every.reshape(-1, 2, width_local)
    dots = jnp.dot(every[:, 0], every[:, 1].T, preferred_element_type=jnp.float32)
    every_f32 = every.astype(jnp.float32)
    norms = jnp.sum(every_f32 * every_f32, axis=-1).T
    part = jnp.concatenate([dots, norms], axis=0)
    parts = [part] + [swap_tensor(part, k) for k in range(1, tensor_size)]
    total = (parts[0] + parts[1]) + (parts[2] + parts[3])
    pairs = dots.shape[0]
    scales = lax.rsqrt(total[pairs:] + EPS)
    sim = SCORE_SCALE * total[:pairs] * scales[0][:, None] * scales[1][None, :]
    row_lse = jax.nn.logsumexp(sim, axis=1)
    col_lse = jax.nn.logsumexp(sim, axis=0)
    positive = jnp.sum(jnp.where(jnp.eye(pairs, dtype=bool), sim, 0.0), axis=0)
    all_loss = 0.5 * (row_lse + col_lse) - positive
    loss = jnp.mean(all_loss)
    pair_loss = lax.dynamic_slice_in_dim(all_loss, dp_at * pair_count, pair_count)
    own_scale = lax.dynamic_slice_in_dim(scales, dp_at * pair_count, pair_count, axis=1)
    embeddings = (mixed.reshape(pair_count, 2, width_local) * own_scale.T[:, :, None]).astype(
        jnp.bfloat16
    )
    return (embeddings, pair_loss, loss)


def solution(mesh):
    in_specs = (
        P("dp", None, None, "tensor"),
        P("dp", None),
        P(),
        P(),
        P(),
        P("dp", "tensor"),
        P("dp", "tensor"),
        P("dp", "tensor"),
    )
    out_specs = (P("dp", None, "tensor"), P("dp"), P())
    return jax.shard_map(body, mesh=mesh, in_specs=in_specs, out_specs=out_specs, check_vma=False)
```

```python
import math

import jax
import jax.numpy as jnp
from jax import lax
from jax.experimental import pallas as pl
from jax.experimental.pallas import tpu as pltpu
from jax.sharding import PartitionSpec as P

HEAD_DIM = 128
EPS = 1e-06
SCORE_SCALE = 20.0

Y, XLO, Z = 4, 2, 8
XHI, CORES = 2, 2
GROUPS = Y * XLO
Z_GROUPS = [[g * Z + z for z in range(Z)] for g in range(GROUPS)]


def rms_rows(values):
    return values * lax.rsqrt(jnp.mean(values * values, axis=-1, keepdims=True) + EPS)


def shift(array, dx=0, dy=0, dz=0):
    pairs = []
    for y in range(Y):
        for x in range(XHI * XLO):
            for z in range(Z):
                for core in range(CORES):

                    def at(x, y, z):
                        x_hi, x_lo = divmod(x, XLO)
                        dp = (y * XLO + x_lo) * Z + z
                        return dp * (XHI * CORES) + x_hi * CORES + core

                    there = at((x + dx) % (XHI * XLO), (y + dy) % Y, (z + dz) % Z)
                    pairs.append((at(x, y, z), there))
    return lax.ppermute(array, ("dp", "tensor"), pairs)


def swap_tensor(array, mask):
    size = XHI * CORES
    return lax.ppermute(array, "tensor", [(i, i ^ mask) for i in range(size)])


def swap_x_lo(array):
    pairs = [(i, (i // Z ^ 1) * Z + i % Z) for i in range(GROUPS * Z)]
    return lax.ppermute(array, "dp", pairs)


def exchange(chunks, groups):
    return lax.all_to_all(
        chunks, "dp", split_axis=0, concat_axis=0, tiled=True, axis_index_groups=groups
    )


def take_last_kernel(len_ref, hidden_ref, out_ref, tile_ref, sem):
    seq_count, depth, width = tile_ref.shape
    spots = [len_ref[seq // 2, seq % 2] - 1 for seq in range(seq_count)]
    copies = []
    for seq, spot in enumerate(spots):
        rows = pl.ds(pl.multiple_of(spot & -depth, depth), depth)
        copies.append(
            pltpu.make_async_copy(hidden_ref.at[seq, rows, :], tile_ref.at[seq], sem.at[seq])
        )
        copies[-1].start()
    row_at = lax.broadcasted_iota(jnp.int32, (depth, width), 0)
    seq_at = lax.broadcasted_iota(jnp.int32, (seq_count, width), 0)
    rows = jnp.zeros((seq_count, width), jnp.float32)
    for seq, spot in enumerate(spots):
        copies[seq].wait()
        tile = tile_ref[seq].astype(jnp.float32)
        row = jnp.sum(jnp.where(row_at == (spot & (depth - 1)), tile, 0.0), axis=0, keepdims=True)
        rows = jnp.where(seq_at == seq, row, rows)
    out_ref[...] = rows.astype(jnp.bfloat16)


def payload_kernel(
    at_ref, r0, r1, r2, r3, gain_ref, kv_ref, other_ref, out_ref, raw_ref, row_ref
):
    y_at, x_lo_at, tensor_at = at_ref[0], at_ref[1], at_ref[2]
    refs = [r0, r1, r2, r3]
    seq_count, width = r0.shape
    rows = width // (XLO * Z)
    squares = None
    for k, ref in enumerate(refs):
        x = ref[...].astype(jnp.float32)
        raw_ref[k] = x
        part = jnp.sum(x * x, axis=-1, keepdims=True)
        squares = part if squares is None else squares + part
    scale = lax.rsqrt(squares / (len(refs) * width) + EPS)
    row_ref[...] = jnp.zeros_like(row_ref)
    for step in range(Y):
        slice_at = (y_at + step) & (Y - 1)
        normed = raw_ref[slice_at ^ tensor_at] * scale * gain_ref[
            :, pl.ds(pl.multiple_of(slice_at * width, width), width)
        ]
        normed = normed.astype(jnp.bfloat16).astype(jnp.float32)
        halves = [normed[:, : Z * rows], normed[:, Z * rows :]]
        for x in range(XLO):
            half = jnp.where(x_lo_at == x, halves[0], halves[1])
            for z in range(Z):
                at = (step * XLO + x) * rows
                row_ref[z, :seq_count, at : at + rows] = half[:, z * rows : (z + 1) * rows]
    depth = kv_ref.shape[0]
    for z in range(Z):
        out_ref[z, :depth, :] = kv_ref[...]
        out_ref[z, depth : XLO * depth, :] = other_ref[...]
        out_ref[z, XLO * depth :, :] = row_ref[z].astype(jnp.bfloat16)


def query_kernel(rows_ref, w0, w1, w2, w3, out_ref, acc_ref):
    depth, _ = w0.shape
    rows = rows_ref[...].astype(jnp.float32)
    total = None
    for step, w_ref in enumerate([w0, w1, w2, w3]):
        lhs = rows[:, :8, step * depth : (step + 1) * depth].reshape(Z * 8, depth)
        part = jnp.dot(lhs.astype(jnp.bfloat16), w_ref[...], preferred_element_type=jnp.float32)
        total = part if total is None else total + part
    high = total.astype(jnp.bfloat16).astype(jnp.float32)
    low = (total - high).astype(jnp.bfloat16).astype(jnp.float32)
    both = high + pltpu.roll(low, 4, 0)
    for head in range(both.shape[1] // HEAD_DIM):
        block = both[:, head * HEAD_DIM : (head + 1) * HEAD_DIM]
        acc_ref[:, head * 8 : (head + 1) * 8, :] = block.reshape(Z, 8, HEAD_DIM)
    out_ref[...] = acc_ref[...].astype(jnp.bfloat16)


def kv_attend_kernel(
    at_ref,
    len_ref,
    x0_ref,
    x1_ref,
    x2_ref,
    x3_ref,
    own_ref,
    up_low_ref,
    up_high_ref,
    down_low_ref,
    down_high_ref,
    far_low_ref,
    far_high_ref,
    part_q_ref,
    gain_ref,
    qg_ref,
    kg_ref,
    out_ref,
    wk_ref,
    wv_ref,
    query_ref,
    sem,
):
    x_refs = [x0_ref, x1_ref, x2_ref, x3_ref]
    _, slots, width = x0_ref.shape
    slices = len(x_refs)
    rows = width // (XLO * Z)
    seq = pl.program_id(0)
    heads = out_ref.shape[1]
    y_at, x_lo_at, tensor_at = at_ref[0], at_ref[1], at_ref[2]

    @pl.when(seq == 0)
    def _():
        for step, halves in enumerate(
            [
                [own_ref],
                [up_low_ref, up_high_ref],
                [far_low_ref, far_high_ref],
                [down_low_ref, down_high_ref],
            ]
        ):
            y = (y_at + step) & (Y - 1)
            for half, piece in enumerate(halves):
                zs = pl.ds(half * (Z // 2), piece.shape[0])
                for x in range(XLO):
                    block = pl.ds(x * rows, rows)
                    for i, w_ref in enumerate([wk_ref, wv_ref]):
                        columns = pl.ds(i * 2 * HEAD_DIM, 2 * HEAD_DIM)
                        pltpu.make_async_copy(
                            piece.at[:, block, columns],
                            w_ref.at[y, x_lo_at ^ x, zs],
                            sem.at[i],
                        ).start()

    squares = None
    for k in range(slices):
        x = x_refs[k][0].astype(jnp.float32)
        part = jnp.sum(x * x, axis=-1, keepdims=True)
        squares = part if squares is None else squares + part
    scale = lax.rsqrt(squares / (slices * width) + EPS)

    @pl.when(seq == 0)
    def _():
        for i, w_ref in enumerate([wk_ref, wv_ref]):
            pltpu.make_async_copy(w_ref, w_ref, sem.at[i]).wait()
        parts = jnp.sum(part_q_ref[...].astype(jnp.float32), axis=0)
        query_ref[...] = parts + pltpu.roll(parts, parts.shape[0] - 4, 0)

    key_proj = value_proj = None
    for k in range(slices):
        x = x_refs[k][0].astype(jnp.float32)
        slice_at = tensor_at ^ k
        at = pl.ds(pl.multiple_of(slice_at * width, width), width)
        normed = (x * scale * gain_ref[:, at]).astype(jnp.bfloat16)
        wk = wk_ref[slice_at].reshape(width, -1)
        wv = wv_ref[slice_at].reshape(width, -1)
        kp = jnp.dot(normed, wk, preferred_element_type=jnp.float32)
        vp = jnp.dot(normed, wv, preferred_element_type=jnp.float32)
        key_proj = kp if key_proj is None else key_proj + kp
        value_proj = vp if value_proj is None else value_proj + vp
    query = query_ref[pl.ds(seq, heads, stride=8), :]
    query = (rms_rows(query) * qg_ref[...]).astype(jnp.bfloat16)
    first = lax.broadcasted_iota(jnp.int32, (heads, 1), 0) < heads // 2
    scores = []
    for h in range(2):
        key = key_proj[:, h * HEAD_DIM : (h + 1) * HEAD_DIM]
        key = (rms_rows(key) * kg_ref[...]).astype(jnp.bfloat16)
        scores.append(
            lax.dot_general(
                query, key, (((1,), (1,)), ((), ())), preferred_element_type=jnp.float32
            )
        )
    scores = jnp.where(first, scores[0], scores[1]) / math.sqrt(HEAD_DIM)
    positions = lax.broadcasted_iota(jnp.int32, (1, slots), 1)
    scores = jnp.where(positions < len_ref[seq >> 1, seq & 1], scores, -1e30)
    expo = jnp.exp(scores - jnp.max(scores, axis=-1, keepdims=True))
    weights = (expo / jnp.sum(expo, axis=-1, keepdims=True)).astype(jnp.bfloat16)
    value = value_proj.astype(jnp.bfloat16)
    mixed = jnp.dot(weights, value, preferred_element_type=jnp.float32)
    out_ref[0] = jnp.where(first, mixed[:, :HEAD_DIM], mixed[:, HEAD_DIM:])


SMEM = pl.BlockSpec(memory_space=pltpu.SMEM)
VMEM = pl.BlockSpec(memory_space=pltpu.VMEM)
ANY = pl.BlockSpec(memory_space=pl.ANY)


def take_last_call(lengths, own):
    seq_count, _, width = own.shape
    return pl.pallas_call(
        take_last_kernel,
        in_specs=[SMEM, pl.BlockSpec(memory_space=pl.ANY)],
        out_specs=VMEM,
        out_shape=jax.ShapeDtypeStruct((seq_count, width), own.dtype),
        scratch_shapes=[
            pltpu.VMEM((seq_count, 16, width), own.dtype),
            pltpu.SemaphoreType.DMA((seq_count,)),
        ],
    )(lengths, own)


def payload_call(at, raw, gains, kv_own, kv_other):
    seq_count, width = raw[0].shape
    rows, columns = kv_own.shape
    return pl.pallas_call(
        payload_kernel,
        in_specs=[SMEM] + [VMEM] * (len(raw) + 3),
        out_specs=VMEM,
        out_shape=jax.ShapeDtypeStruct((Z, XLO * rows + 16, columns), jnp.bfloat16),
        scratch_shapes=[
            pltpu.VMEM((len(raw), seq_count, width), jnp.float32),
            pltpu.VMEM((Z, 16, columns), jnp.float32),
        ],
    )(at, *raw, gains, kv_own, kv_other)


def query_call(z_all, rest):
    shape = (Z, (rest[0].shape[1] // HEAD_DIM) * 8, HEAD_DIM)
    tail = z_all.shape[1] // 16 - 1
    return pl.pallas_call(
        query_kernel,
        grid=(1,),
        in_specs=[pl.BlockSpec((Z, 16, z_all.shape[2]), lambda i: (0, tail, 0))]
        + [VMEM] * len(rest),
        out_specs=VMEM,
        out_shape=jax.ShapeDtypeStruct(shape, jnp.bfloat16),
        scratch_shapes=[pltpu.VMEM(shape, jnp.float32)],
    )(z_all, *rest)


def kv_attend(at, lengths, slices, pieces, partial_q, gains, qg, kg):
    seq_count, slots, width = slices[0].shape
    model_width = gains.size
    heads = partial_q.shape[1] // 8
    kv_width = 2 * HEAD_DIM
    rows = model_width // (Y * XLO * Z)
    x_spec = pl.BlockSpec((1, slots, width), lambda seq: (seq, 0, 0))
    return pl.pallas_call(
        kv_attend_kernel,
        grid=(seq_count,),
        in_specs=[SMEM, SMEM]
        + [x_spec] * len(slices)
        + [pl.BlockSpec(memory_space=pltpu.HBM)] * len(pieces)
        + [VMEM] * 4,
        out_specs=pl.BlockSpec((1, heads, HEAD_DIM), lambda seq: (seq, 0, 0)),
        out_shape=jax.ShapeDtypeStruct((seq_count, heads, HEAD_DIM), jnp.float32),
        scratch_shapes=[pltpu.VMEM((Y, XLO, Z, rows, kv_width), jnp.bfloat16)] * 2
        + [
            pltpu.VMEM((heads * 8, HEAD_DIM), jnp.float32),
            pltpu.SemaphoreType.DMA((2,)),
        ],
        compiler_params=pltpu.CompilerParams(vmem_limit_bytes=58 * 1024 * 1024),
        cost_estimate=pl.CostEstimate(
            flops=4 * seq_count * slots * model_width * kv_width,
            bytes_accessed=2 * seq_count * slots * model_width + 4 * model_width * kv_width,
            transcendentals=seq_count * heads * slots,
        ),
    )(at, lengths, *slices, *pieces, partial_q, gains, qg, kg)


def body(
    hidden, lengths, norm_gain, q_norm_gain, k_norm_gain, query_weight, key_weight, value_weight
):
    tensor_size = lax.axis_size("tensor")
    tensor_at = lax.axis_index("tensor")
    dp_at = lax.axis_index("dp")
    x_lo_at = (dp_at >> (Z.bit_length() - 1)) & (XLO - 1)
    y_at = dp_at >> ((Z * XLO).bit_length() - 1)
    at = jnp.stack([y_at, x_lo_at, tensor_at]).astype(jnp.int32)

    pair_count, _, seq_slots, width_local = hidden.shape
    seq_count = 2 * pair_count
    own = hidden.reshape(seq_count, seq_slots, width_local)
    gains = norm_gain[None]

    kv_weight = jnp.concatenate([key_weight, value_weight], axis=1)
    kv_other = swap_x_lo(kv_weight)
    query_other = swap_x_lo(query_weight)
    last_own = take_last_call(lengths, own)
    last_raw = [last_own] + [swap_tensor(last_own, k) for k in range(1, tensor_size)]

    sent_own = lax.optimization_barrier((own, kv_other, query_other, *last_raw))[0]
    far = swap_tensor(sent_own, 2)
    peer = swap_tensor(sent_own, 1)

    payload = payload_call(at, last_raw, gains, kv_weight, kv_other)
    payload, _ = lax.optimization_barrier((payload, query_other))
    z_all = exchange(payload, Z_GROUPS)

    rest = jnp.concatenate([query_weight, query_other])
    rest = [rest] + [shift(rest, dy=-step) for step in range(1, Y)]

    z_sent = lax.optimization_barrier((z_all, *rest))[0][:, :-16]
    z_low, z_high = z_sent[: Z // 2], z_sent[Z // 2 :]
    up_low = shift(z_low, dy=-1)
    down_high = shift(z_high, dy=1)
    up_high = shift(z_high, dy=-1)
    down_low = shift(z_low, dy=1)
    far_low = shift(up_low, dy=-1)
    far_high = shift(down_high, dy=1)
    pieces = [z_all, up_low, up_high, down_low, down_high, far_low, far_high]

    partial_q = exchange(query_call(z_all, rest), Z_GROUPS)
    far_peer = swap_tensor(lax.optimization_barrier((far, up_low, down_high, up_high, down_low))[0], 1)

    mixed = kv_attend(
        at,
        lengths,
        [own, peer, far, far_peer],
        pieces,
        partial_q,
        gains,
        q_norm_gain[None],
        k_norm_gain[None],
    ).reshape(seq_count, width_local)

    sent = mixed.astype(jnp.bfloat16)
    every = exchange(jnp.broadcast_to(sent[None], (GROUPS * Z,) + sent.shape), None)
    every = every.reshape(-1, 2, width_local)
    dots = jnp.dot(every[:, 0], every[:, 1].T, preferred_element_type=jnp.float32)
    every_f32 = every.astype(jnp.float32)
    norms = jnp.sum(every_f32 * every_f32, axis=-1).T
    part = jnp.concatenate([dots, norms], axis=0)
    parts = [part] + [swap_tensor(part, k) for k in range(1, tensor_size)]
    total = (parts[0] + parts[1]) + (parts[2] + parts[3])
    pairs = dots.shape[0]
    scales = lax.rsqrt(total[pairs:] + EPS)
    sim = SCORE_SCALE * total[:pairs] * scales[0][:, None] * scales[1][None, :]
    row_lse = jax.nn.logsumexp(sim, axis=1)
    col_lse = jax.nn.logsumexp(sim, axis=0)
    positive = jnp.sum(jnp.where(jnp.eye(pairs, dtype=bool), sim, 0.0), axis=0)
    all_loss = 0.5 * (row_lse + col_lse) - positive
    loss = jnp.mean(all_loss)
    pair_loss = lax.dynamic_slice_in_dim(all_loss, dp_at * pair_count, pair_count)
    own_scale = lax.dynamic_slice_in_dim(scales, dp_at * pair_count, pair_count, axis=1)
    embeddings = (mixed.reshape(pair_count, 2, width_local) * own_scale.T[:, :, None]).astype(
        jnp.bfloat16
    )
    return (embeddings, pair_loss, loss)


def solution(mesh):
    in_specs = (
        P("dp", None, None, "tensor"),
        P("dp", None),
        P(),
        P(),
        P(),
        P("dp", "tensor"),
        P("dp", "tensor"),
        P("dp", "tensor"),
    )
    out_specs = (P("dp", None, "tensor"), P("dp"), P())
    return jax.shard_map(body, mesh=mesh, in_specs=in_specs, out_specs=out_specs, check_vma=False)
```

```python
import math

import jax
import jax.numpy as jnp
from jax import lax
from jax.experimental import pallas as pl
from jax.experimental.pallas import tpu as pltpu
from jax.sharding import PartitionSpec as P

HEAD_DIM = 128
EPS = 1e-06
SCORE_SCALE = 20.0

Y, XLO, Z = 4, 2, 8
XHI, CORES = 2, 2
GROUPS = Y * XLO
Z_GROUPS = [[g * Z + z for z in range(Z)] for g in range(GROUPS)]


def rms_rows(values):
    return values * lax.rsqrt(jnp.mean(values * values, axis=-1, keepdims=True) + EPS)


def shift(array, dx=0, dy=0, dz=0):
    pairs = []
    for y in range(Y):
        for x in range(XHI * XLO):
            for z in range(Z):
                for core in range(CORES):

                    def at(x, y, z):
                        x_hi, x_lo = divmod(x, XLO)
                        dp = (y * XLO + x_lo) * Z + z
                        return dp * (XHI * CORES) + x_hi * CORES + core

                    there = at((x + dx) % (XHI * XLO), (y + dy) % Y, (z + dz) % Z)
                    pairs.append((at(x, y, z), there))
    return lax.ppermute(array, ("dp", "tensor"), pairs)


def swap_tensor(array, mask):
    size = XHI * CORES
    return lax.ppermute(array, "tensor", [(i, i ^ mask) for i in range(size)])


def swap_x_lo(array):
    pairs = [(i, (i // Z ^ 1) * Z + i % Z) for i in range(GROUPS * Z)]
    return lax.ppermute(array, "dp", pairs)


def exchange(chunks, groups):
    return lax.all_to_all(
        chunks, "dp", split_axis=0, concat_axis=0, tiled=True, axis_index_groups=groups
    )


def take_last_kernel(len_ref, hidden_ref, out_ref, tile_ref, sem):
    seq_count, depth, width = tile_ref.shape
    spots = [len_ref[seq // 2, seq % 2] - 1 for seq in range(seq_count)]
    copies = []
    for seq, spot in enumerate(spots):
        rows = pl.ds(pl.multiple_of(spot & -depth, depth), depth)
        copies.append(
            pltpu.make_async_copy(hidden_ref.at[seq, rows, :], tile_ref.at[seq], sem.at[seq])
        )
        copies[-1].start()
    row_at = lax.broadcasted_iota(jnp.int32, (depth, width), 0)
    seq_at = lax.broadcasted_iota(jnp.int32, (seq_count, width), 0)
    rows = jnp.zeros((seq_count, width), jnp.float32)
    for seq, spot in enumerate(spots):
        copies[seq].wait()
        tile = tile_ref[seq].astype(jnp.float32)
        row = jnp.sum(jnp.where(row_at == (spot & (depth - 1)), tile, 0.0), axis=0, keepdims=True)
        rows = jnp.where(seq_at == seq, row, rows)
    out_ref[...] = rows.astype(jnp.bfloat16)


def last_rows_kernel(at_ref, r0, r1, r2, r3, gain_ref, out_ref, raw_ref, row_ref):
    y_at, x_lo_at, tensor_at = at_ref[0], at_ref[1], at_ref[2]
    refs = [r0, r1, r2, r3]
    seq_count, width = r0.shape
    rows = width // (XLO * Z)
    squares = None
    for k, ref in enumerate(refs):
        x = ref[...].astype(jnp.float32)
        raw_ref[k] = x
        part = jnp.sum(x * x, axis=-1, keepdims=True)
        squares = part if squares is None else squares + part
    scale = lax.rsqrt(squares / (len(refs) * width) + EPS)
    row_ref[...] = jnp.zeros_like(row_ref)
    for step in range(Y):
        slice_at = (y_at + step) & (Y - 1)
        normed = raw_ref[slice_at ^ tensor_at] * scale * gain_ref[
            :, pl.ds(pl.multiple_of(slice_at * width, width), width)
        ]
        normed = normed.astype(jnp.bfloat16).astype(jnp.float32)
        halves = [normed[:, : Z * rows], normed[:, Z * rows :]]
        row, lane = (0, step * XLO * rows) if step < Y - 1 else (8, 0)
        for x in range(XLO):
            half = jnp.where(x_lo_at == x, halves[0], halves[1])
            for z in range(Z):
                at = lane + x * rows
                row_ref[z, row : row + seq_count, at : at + rows] = half[
                    :, z * rows : (z + 1) * rows
                ]
    out_ref[...] = row_ref[...].astype(jnp.bfloat16)


def query_kernel(rows_ref, w0, w1, w2, w3, out_ref, acc_ref):
    depth, _ = w0.shape
    rows = rows_ref[...].astype(jnp.float32)
    total = None
    for step, w_ref in enumerate([w0, w1, w2, w3]):
        row, lane = (0, step * depth) if step < Y - 1 else (8, 0)
        lhs = rows[:, row : row + 8, lane : lane + depth].reshape(Z * 8, depth)
        part = jnp.dot(
            lhs.astype(jnp.bfloat16), w_ref[:, HEAD_DIM:], preferred_element_type=jnp.float32
        )
        total = part if total is None else total + part
    high = total.astype(jnp.bfloat16).astype(jnp.float32)
    low = (total - high).astype(jnp.bfloat16).astype(jnp.float32)
    both = high + pltpu.roll(low, 4, 0)
    for head in range(both.shape[1] // HEAD_DIM):
        block = both[:, head * HEAD_DIM : (head + 1) * HEAD_DIM]
        acc_ref[:, head * 8 : (head + 1) * 8, :] = block.reshape(Z, 8, HEAD_DIM)
    out_ref[...] = acc_ref[...].astype(jnp.bfloat16)


def kv_attend_kernel(
    at_ref,
    len_ref,
    x0_ref,
    x1_ref,
    x2_ref,
    x3_ref,
    own_ref,
    up_ref,
    down_ref,
    far_low_ref,
    far_high_ref,
    last_ref,
    gain_ref,
    qg_ref,
    kg_ref,
    out_ref,
    wk_ref,
    wv_ref,
    parts_ref,
    query_ref,
    sem,
):
    x_refs = [x0_ref, x1_ref, x2_ref, x3_ref]
    _, slots, width = x0_ref.shape
    slices = len(x_refs)
    rows = width // (XLO * Z)
    seq = pl.program_id(0)
    heads = out_ref.shape[1]
    y_at, x_lo_at, tensor_at = at_ref[0], at_ref[1], at_ref[2]

    @pl.when(seq == 0)
    def _():
        low = Z // 2

        def start(source, target, at):
            pltpu.make_async_copy(source, target, sem.at[at]).start()

        start(last_ref.at[:, pl.ds(Y * XLO * rows, parts_ref.shape[1]), :], parts_ref, 2)
        for step, halves in enumerate(
            [[own_ref], [up_ref], [far_low_ref, far_high_ref], [down_ref]]
        ):
            y = (y_at + step) & (Y - 1)
            for x in range(XLO):
                block = pl.ds(x * rows, rows)
                for half, piece in enumerate(halves):
                    zs = pl.ds(half * low, piece.shape[0])
                    wk_at = wk_ref.at[y, x_lo_at ^ x, zs]
                    start(piece.at[:, block, pl.ds(0, 2 * HEAD_DIM)], wk_at, 0)
                    wv_at = wv_ref.at[y, x_lo_at ^ x, zs, :, pl.ds(0, HEAD_DIM)]
                    start(piece.at[:, block, pl.ds(2 * HEAD_DIM, HEAD_DIM)], wv_at, 1)
                block = pl.ds((step * XLO + x) * rows, rows)
                wv_at = wv_ref.at[y, x_lo_at ^ x, :, :, pl.ds(HEAD_DIM, HEAD_DIM)]
                start(last_ref.at[:, block, :], wv_at, 1)

    squares = None
    for k in range(slices):
        x = x_refs[k][0].astype(jnp.float32)
        part = jnp.sum(x * x, axis=-1, keepdims=True)
        squares = part if squares is None else squares + part
    scale = lax.rsqrt(squares / (slices * width) + EPS)

    @pl.when(seq == 0)
    def _():
        for at, ref in enumerate([wk_ref, wv_ref, parts_ref]):
            pltpu.make_async_copy(ref, ref, sem.at[at]).wait()
        parts = jnp.sum(parts_ref[...].astype(jnp.float32), axis=0)
        query_ref[...] = parts + pltpu.roll(parts, parts.shape[0] - 4, 0)

    key_proj = value_proj = None
    for k in range(slices):
        x = x_refs[k][0].astype(jnp.float32)
        slice_at = tensor_at ^ k
        at = pl.ds(pl.multiple_of(slice_at * width, width), width)
        normed = (x * scale * gain_ref[:, at]).astype(jnp.bfloat16)
        wk = wk_ref[slice_at].reshape(width, -1)
        wv = wv_ref[slice_at].reshape(width, -1)
        kp = jnp.dot(normed, wk, preferred_element_type=jnp.float32)
        vp = jnp.dot(normed, wv, preferred_element_type=jnp.float32)
        key_proj = kp if key_proj is None else key_proj + kp
        value_proj = vp if value_proj is None else value_proj + vp
    query = query_ref[pl.ds(seq, heads, stride=8), :]
    query = (rms_rows(query) * qg_ref[...]).astype(jnp.bfloat16)
    first = lax.broadcasted_iota(jnp.int32, (heads, 1), 0) < heads // 2
    scores = []
    for h in range(2):
        key = key_proj[:, h * HEAD_DIM : (h + 1) * HEAD_DIM]
        key = (rms_rows(key) * kg_ref[...]).astype(jnp.bfloat16)
        scores.append(
            lax.dot_general(
                query, key, (((1,), (1,)), ((), ())), preferred_element_type=jnp.float32
            )
        )
    scores = jnp.where(first, scores[0], scores[1]) / math.sqrt(HEAD_DIM)
    positions = lax.broadcasted_iota(jnp.int32, (1, slots), 1)
    scores = jnp.where(positions < len_ref[seq >> 1, seq & 1], scores, -1e30)
    expo = jnp.exp(scores - jnp.max(scores, axis=-1, keepdims=True))
    weights = (expo / jnp.sum(expo, axis=-1, keepdims=True)).astype(jnp.bfloat16)
    value = value_proj.astype(jnp.bfloat16)
    mixed = jnp.dot(weights, value, preferred_element_type=jnp.float32)
    out_ref[0] = jnp.where(first, mixed[:, :HEAD_DIM], mixed[:, HEAD_DIM:])


SMEM = pl.BlockSpec(memory_space=pltpu.SMEM)
VMEM = pl.BlockSpec(memory_space=pltpu.VMEM)


def take_last_call(lengths, own):
    seq_count, _, width = own.shape
    return pl.pallas_call(
        take_last_kernel,
        in_specs=[SMEM, pl.BlockSpec(memory_space=pl.ANY)],
        out_specs=VMEM,
        out_shape=jax.ShapeDtypeStruct((seq_count, width), own.dtype),
        scratch_shapes=[
            pltpu.VMEM((seq_count, 16, width), own.dtype),
            pltpu.SemaphoreType.DMA((seq_count,)),
        ],
    )(lengths, own)


def last_rows_call(at, raw, gains):
    seq_count, width = raw[0].shape
    shape = (Z, 16, (Y - 1) * XLO * (width // (XLO * Z)))
    return pl.pallas_call(
        last_rows_kernel,
        in_specs=[SMEM] + [VMEM] * (len(raw) + 1),
        out_specs=VMEM,
        out_shape=jax.ShapeDtypeStruct(shape, jnp.bfloat16),
        scratch_shapes=[
            pltpu.VMEM((len(raw), seq_count, width), jnp.float32),
            pltpu.VMEM(shape, jnp.float32),
        ],
    )(at, *raw, gains)


def query_call(z_all, rest):
    shape = (Z, (rest[0].shape[1] // HEAD_DIM - 1) * 8, HEAD_DIM)
    tail = z_all.shape[1] // 16 - 1
    return pl.pallas_call(
        query_kernel,
        grid=(1,),
        in_specs=[pl.BlockSpec((Z, 16, z_all.shape[2]), lambda i: (0, tail, 0))]
        + [VMEM] * len(rest),
        out_specs=VMEM,
        out_shape=jax.ShapeDtypeStruct(shape, jnp.bfloat16),
        scratch_shapes=[pltpu.VMEM(shape, jnp.float32)],
    )(z_all, *rest)


def kv_attend(at, lengths, slices, pieces, last, gains, heads, qg, kg):
    seq_count, slots, width = slices[0].shape
    model_width = gains.size
    kv_width = 2 * HEAD_DIM
    rows = model_width // (Y * XLO * Z)
    x_spec = pl.BlockSpec((1, slots, width), lambda seq: (seq, 0, 0))
    return pl.pallas_call(
        kv_attend_kernel,
        grid=(seq_count,),
        in_specs=[SMEM, SMEM]
        + [x_spec] * len(slices)
        + [pl.BlockSpec(memory_space=pltpu.HBM)] * (len(pieces) + 1)
        + [VMEM] * 3,
        out_specs=pl.BlockSpec((1, heads, HEAD_DIM), lambda seq: (seq, 0, 0)),
        out_shape=jax.ShapeDtypeStruct((seq_count, heads, HEAD_DIM), jnp.float32),
        scratch_shapes=[pltpu.VMEM((Y, XLO, Z, rows, kv_width), jnp.bfloat16)] * 2
        + [
            pltpu.VMEM((Z, heads * 8, HEAD_DIM), jnp.bfloat16),
            pltpu.VMEM((heads * 8, HEAD_DIM), jnp.float32),
            pltpu.SemaphoreType.DMA((3,)),
        ],
        compiler_params=pltpu.CompilerParams(vmem_limit_bytes=58 * 1024 * 1024),
        cost_estimate=pl.CostEstimate(
            flops=4 * seq_count * slots * model_width * kv_width,
            bytes_accessed=2 * seq_count * slots * model_width + 4 * model_width * kv_width,
            transcendentals=seq_count * heads * slots,
        ),
    )(at, lengths, *slices, *pieces, last, gains, qg, kg)


def body(
    hidden, lengths, norm_gain, q_norm_gain, k_norm_gain, query_weight, key_weight, value_weight
):
    tensor_size = lax.axis_size("tensor")
    tensor_at = lax.axis_index("tensor")
    dp_at = lax.axis_index("dp")
    x_lo_at = (dp_at >> (Z.bit_length() - 1)) & (XLO - 1)
    y_at = dp_at >> ((Z * XLO).bit_length() - 1)
    at = jnp.stack([y_at, x_lo_at, tensor_at]).astype(jnp.int32)

    pair_count, _, seq_slots, width_local = hidden.shape
    seq_count = 2 * pair_count
    own = hidden.reshape(seq_count, seq_slots, width_local)
    rows_local, kv_width = key_weight.shape
    query_width = query_weight.shape[1]
    gains = norm_gain[None]

    kv_weight = jnp.concatenate([key_weight, value_weight], axis=1)
    kv_both = jnp.concatenate([kv_weight, swap_x_lo(kv_weight)])
    query_other = swap_x_lo(query_weight)
    last_own = take_last_call(lengths, own)
    last_raw = [last_own] + [swap_tensor(last_own, k) for k in range(1, tensor_size)]

    sent_own = lax.optimization_barrier((own, kv_both, query_other, *last_raw))[0]
    far = swap_tensor(sent_own, 2)
    peer = swap_tensor(sent_own, 1)

    block = kv_both[:, : kv_width + HEAD_DIM]
    rows = last_rows_call(at, last_raw, gains)
    rows, _ = lax.optimization_barrier((rows, query_other))
    z_all = exchange(
        jnp.concatenate([jnp.broadcast_to(block[None], (Z,) + block.shape), rows], axis=1),
        Z_GROUPS,
    )

    rest = jnp.concatenate(
        [kv_both[:, kv_width + HEAD_DIM :], jnp.concatenate([query_weight, query_other])], axis=1
    )
    rest = [rest] + [shift(rest, dy=-step) for step in range(1, Y)]
    partial_q = query_call(z_all, rest)
    heads = [array[:, :HEAD_DIM] for array in rest]

    z_own, *heads = lax.optimization_barrier((z_all[:, : block.shape[0]], *heads))
    head = jnp.concatenate(heads)
    z_up = shift(z_own, dy=-1)
    z_down = shift(z_own, dy=1)
    far_low = shift(z_up[: Z // 2], dy=-1)
    far_high = shift(z_down[Z // 2 :], dy=1)
    pieces = [z_own, z_up, z_down, far_low, far_high]

    corner = swap_tensor(z_own[:, :16, :HEAD_DIM], 1)
    last = exchange(
        jnp.concatenate(
            [jnp.broadcast_to(head[None], (Z,) + head.shape), partial_q, corner], axis=1
        ),
        Z_GROUPS,
    )
    far_peer = swap_tensor(lax.optimization_barrier((far, z_up, z_down))[0], 1)

    mixed = kv_attend(
        at,
        lengths,
        [own, peer, far, far_peer],
        pieces,
        last,
        gains,
        query_width // HEAD_DIM,
        q_norm_gain[None],
        k_norm_gain[None],
    ).reshape(seq_count, width_local)

    sent = mixed.astype(jnp.bfloat16)
    every = exchange(jnp.broadcast_to(sent[None], (GROUPS * Z,) + sent.shape), None)
    every = every.reshape(-1, 2, width_local)
    dots = jnp.dot(every[:, 0], every[:, 1].T, preferred_element_type=jnp.float32)
    every_f32 = every.astype(jnp.float32)
    norms = jnp.sum(every_f32 * every_f32, axis=-1).T
    part = jnp.concatenate([dots, norms], axis=0)
    parts = [part] + [swap_tensor(part, k) for k in range(1, tensor_size)]
    total = (parts[0] + parts[1]) + (parts[2] + parts[3])
    pairs = dots.shape[0]
    scales = lax.rsqrt(total[pairs:] + EPS)
    sim = SCORE_SCALE * total[:pairs] * scales[0][:, None] * scales[1][None, :]
    row_lse = jax.nn.logsumexp(sim, axis=1)
    col_lse = jax.nn.logsumexp(sim, axis=0)
    positive = jnp.sum(jnp.where(jnp.eye(pairs, dtype=bool), sim, 0.0), axis=0)
    all_loss = 0.5 * (row_lse + col_lse) - positive
    loss = jnp.mean(all_loss)
    pair_loss = lax.dynamic_slice_in_dim(all_loss, dp_at * pair_count, pair_count)
    own_scale = lax.dynamic_slice_in_dim(scales, dp_at * pair_count, pair_count, axis=1)
    embeddings = (mixed.reshape(pair_count, 2, width_local) * own_scale.T[:, :, None]).astype(
        jnp.bfloat16
    )
    return (embeddings, pair_loss, loss)


def solution(mesh):
    in_specs = (
        P("dp", None, None, "tensor"),
        P("dp", None),
        P(),
        P(),
        P(),
        P("dp", "tensor"),
        P("dp", "tensor"),
        P("dp", "tensor"),
    )
    out_specs = (P("dp", None, "tensor"), P("dp"), P())
    return jax.shard_map(body, mesh=mesh, in_specs=in_specs, out_specs=out_specs, check_vma=False)
```

```python
import math

import jax
import jax.numpy as jnp
from jax import lax
from jax.experimental import pallas as pl
from jax.experimental.pallas import tpu as pltpu
from jax.sharding import PartitionSpec as P

HEAD_DIM = 128
EPS = 1e-06
SCORE_SCALE = 20.0

Y, XLO, Z = 4, 2, 8
XHI, CORES = 2, 2
GROUPS = Y * XLO
Z_GROUPS = [[g * Z + z for z in range(Z)] for g in range(GROUPS)]


def rms_rows(values):
    return values * lax.rsqrt(jnp.mean(values * values, axis=-1, keepdims=True) + EPS)


def shift(array, dx=0, dy=0, dz=0):
    pairs = []
    for y in range(Y):
        for x in range(XHI * XLO):
            for z in range(Z):
                for core in range(CORES):

                    def at(x, y, z):
                        x_hi, x_lo = divmod(x, XLO)
                        dp = (y * XLO + x_lo) * Z + z
                        return dp * (XHI * CORES) + x_hi * CORES + core

                    there = at((x + dx) % (XHI * XLO), (y + dy) % Y, (z + dz) % Z)
                    pairs.append((at(x, y, z), there))
    return lax.ppermute(array, ("dp", "tensor"), pairs)


def swap_tensor(array, mask):
    size = XHI * CORES
    return lax.ppermute(array, "tensor", [(i, i ^ mask) for i in range(size)])


def swap_x_lo(array):
    pairs = [(i, (i // Z ^ 1) * Z + i % Z) for i in range(GROUPS * Z)]
    return lax.ppermute(array, "dp", pairs)


def exchange(chunks, groups):
    return lax.all_to_all(
        chunks, "dp", split_axis=0, concat_axis=0, tiled=True, axis_index_groups=groups
    )


def take_last_kernel(len_ref, hidden_ref, out_ref, tile_ref, sem):
    seq_count, depth, width = tile_ref.shape
    spots = [len_ref[seq // 2, seq % 2] - 1 for seq in range(seq_count)]
    copies = []
    for seq, spot in enumerate(spots):
        rows = pl.ds(pl.multiple_of(spot & -depth, depth), depth)
        copies.append(
            pltpu.make_async_copy(hidden_ref.at[seq, rows, :], tile_ref.at[seq], sem.at[seq])
        )
        copies[-1].start()
    row_at = lax.broadcasted_iota(jnp.int32, (depth, width), 0)
    seq_at = lax.broadcasted_iota(jnp.int32, (seq_count, width), 0)
    rows = jnp.zeros((seq_count, width), jnp.float32)
    for seq, spot in enumerate(spots):
        copies[seq].wait()
        tile = tile_ref[seq].astype(jnp.float32)
        row = jnp.sum(jnp.where(row_at == (spot & (depth - 1)), tile, 0.0), axis=0, keepdims=True)
        rows = jnp.where(seq_at == seq, row, rows)
    out_ref[...] = rows.astype(jnp.bfloat16)


def last_rows_kernel(at_ref, r0, r1, r2, r3, gain_ref, out_ref, raw_ref, row_ref):
    y_at, x_lo_at, tensor_at = at_ref[0], at_ref[1], at_ref[2]
    refs = [r0, r1, r2, r3]
    seq_count, width = r0.shape
    rows = width // (XLO * Z)
    squares = None
    for k, ref in enumerate(refs):
        x = ref[...].astype(jnp.float32)
        raw_ref[k] = x
        part = jnp.sum(x * x, axis=-1, keepdims=True)
        squares = part if squares is None else squares + part
    scale = lax.rsqrt(squares / (len(refs) * width) + EPS)
    row_ref[...] = jnp.zeros_like(row_ref)
    for step in range(Y):
        slice_at = (y_at + step) & (Y - 1)
        normed = raw_ref[slice_at ^ tensor_at] * scale * gain_ref[
            :, pl.ds(pl.multiple_of(slice_at * width, width), width)
        ]
        normed = normed.astype(jnp.bfloat16).astype(jnp.float32)
        halves = [normed[:, : Z * rows], normed[:, Z * rows :]]
        row, lane = (0, step * XLO * rows) if step < Y - 1 else (8, 0)
        for x in range(XLO):
            half = jnp.where(x_lo_at == x, halves[0], halves[1])
            for z in range(Z):
                at = lane + x * rows
                row_ref[z, row : row + seq_count, at : at + rows] = half[
                    :, z * rows : (z + 1) * rows
                ]
    out_ref[...] = row_ref[...].astype(jnp.bfloat16)


def second_payload_kernel(rows_ref, w0, w1, w2, w3, out_ref, acc_ref):
    depth, _ = w0.shape
    rows = rows_ref[...].astype(jnp.float32)
    total = None
    for step, w_ref in enumerate([w0, w1, w2, w3]):
        row, lane = (0, step * depth) if step < Y - 1 else (8, 0)
        lhs = rows[:, row : row + 8, lane : lane + depth].reshape(Z * 8, depth)
        part = jnp.dot(
            lhs.astype(jnp.bfloat16), w_ref[:, HEAD_DIM:], preferred_element_type=jnp.float32
        )
        total = part if total is None else total + part
    high = total.astype(jnp.bfloat16).astype(jnp.float32)
    low = (total - high).astype(jnp.bfloat16).astype(jnp.float32)
    both = high + pltpu.roll(low, 4, 0)
    for head in range(both.shape[1] // HEAD_DIM):
        block = both[:, head * HEAD_DIM : (head + 1) * HEAD_DIM]
        acc_ref[:, head * 8 : (head + 1) * 8, :] = block.reshape(Z, 8, HEAD_DIM)
    for z in range(Z):
        for step, w_ref in enumerate([w0, w1, w2, w3]):
            out_ref[z, step * depth : (step + 1) * depth, :] = w_ref[:, :HEAD_DIM]
        tail = slice(Y * depth, Y * depth + acc_ref.shape[1])
        out_ref[z, tail, :] = acc_ref[z].astype(jnp.bfloat16)
        out_ref[z, tail.stop :, :] = jnp.zeros((16, HEAD_DIM), jnp.bfloat16)


def kv_attend_kernel(
    at_ref,
    len_ref,
    x0_ref,
    x1_ref,
    x2_ref,
    x3_ref,
    own_ref,
    up_ref,
    down_ref,
    far_low_ref,
    far_high_ref,
    last_ref,
    corner_ref,
    gain_ref,
    qg_ref,
    kg_ref,
    out_ref,
    wk_ref,
    wv_ref,
    parts_ref,
    query_ref,
    sem,
):
    del corner_ref
    x_refs = [x0_ref, x1_ref, x2_ref, x3_ref]
    per_step, slots, width = x0_ref.shape
    slices = len(x_refs)
    rows = width // (XLO * Z)
    step_at = pl.program_id(0)
    heads = out_ref.shape[1]
    y_at, x_lo_at, tensor_at = at_ref[0], at_ref[1], at_ref[2]

    @pl.when(step_at == 0)
    def _():
        low = Z // 2

        def start(source, target, at):
            pltpu.make_async_copy(source, target, sem.at[at]).start()

        start(last_ref.at[:, pl.ds(Y * XLO * rows, parts_ref.shape[1]), :], parts_ref, 2)
        for step, halves in enumerate(
            [[own_ref], [up_ref], [far_low_ref, far_high_ref], [down_ref]]
        ):
            y = (y_at + step) & (Y - 1)
            for x in range(XLO):
                block = pl.ds(x * rows, rows)
                for half, piece in enumerate(halves):
                    zs = pl.ds(half * low, piece.shape[0])
                    wk_at = wk_ref.at[y, x_lo_at ^ x, zs]
                    start(piece.at[:, block, pl.ds(0, 2 * HEAD_DIM)], wk_at, 0)
                    wv_at = wv_ref.at[y, x_lo_at ^ x, zs, :, pl.ds(0, HEAD_DIM)]
                    start(piece.at[:, block, pl.ds(2 * HEAD_DIM, HEAD_DIM)], wv_at, 1)
                block = pl.ds((step * XLO + x) * rows, rows)
                wv_at = wv_ref.at[y, x_lo_at ^ x, :, :, pl.ds(HEAD_DIM, HEAD_DIM)]
                start(last_ref.at[:, block, :], wv_at, 1)

    squares = None
    for k in range(slices):
        x = x_refs[k][...].reshape(-1, width).astype(jnp.float32)
        part = jnp.sum(x * x, axis=-1, keepdims=True)
        squares = part if squares is None else squares + part
    scale = lax.rsqrt(squares / (slices * width) + EPS)

    @pl.when(step_at == 0)
    def _():
        for at, ref in enumerate([wk_ref, wv_ref, parts_ref]):
            pltpu.make_async_copy(ref, ref, sem.at[at]).wait()
        parts = jnp.sum(parts_ref[...].astype(jnp.float32), axis=0)
        query_ref[...] = parts + pltpu.roll(parts, parts.shape[0] - 4, 0)

    key_proj = value_proj = None
    for k in range(slices):
        x = x_refs[k][...].reshape(-1, width).astype(jnp.float32)
        slice_at = tensor_at ^ k
        at = pl.ds(pl.multiple_of(slice_at * width, width), width)
        normed = (x * scale * gain_ref[:, at]).astype(jnp.bfloat16)
        wk = wk_ref[slice_at].reshape(width, -1)
        wv = wv_ref[slice_at].reshape(width, -1)
        kp = jnp.dot(normed, wk, preferred_element_type=jnp.float32)
        vp = jnp.dot(normed, wv, preferred_element_type=jnp.float32)
        key_proj = kp if key_proj is None else key_proj + kp
        value_proj = vp if value_proj is None else value_proj + vp
    first = lax.broadcasted_iota(jnp.int32, (heads, 1), 0) < heads // 2
    positions = lax.broadcasted_iota(jnp.int32, (1, slots), 1)
    keys = []
    for h in range(2):
        key = key_proj[:, h * HEAD_DIM : (h + 1) * HEAD_DIM]
        keys.append((rms_rows(key) * kg_ref[...]).astype(jnp.bfloat16))
    value = value_proj.astype(jnp.bfloat16)
    for j in range(per_step):
        seq = step_at * per_step + j
        own = slice(j * slots, (j + 1) * slots)
        query = query_ref[pl.ds(seq, heads, stride=8), :]
        query = (rms_rows(query) * qg_ref[...]).astype(jnp.bfloat16)
        scores = [
            lax.dot_general(
                query, key[own], (((1,), (1,)), ((), ())), preferred_element_type=jnp.float32
            )
            for key in keys
        ]
        scores = jnp.where(first, scores[0], scores[1]) / math.sqrt(HEAD_DIM)
        scores = jnp.where(positions < len_ref[seq >> 1, seq & 1], scores, -1e30)
        expo = jnp.exp(scores - jnp.max(scores, axis=-1, keepdims=True))
        weights = (expo / jnp.sum(expo, axis=-1, keepdims=True)).astype(jnp.bfloat16)
        mixed = jnp.dot(weights, value[own], preferred_element_type=jnp.float32)
        out_ref[j] = jnp.where(first, mixed[:, :HEAD_DIM], mixed[:, HEAD_DIM:])


SMEM = pl.BlockSpec(memory_space=pltpu.SMEM)
VMEM = pl.BlockSpec(memory_space=pltpu.VMEM)


def take_last_call(lengths, own):
    seq_count, _, width = own.shape
    return pl.pallas_call(
        take_last_kernel,
        in_specs=[SMEM, pl.BlockSpec(memory_space=pl.ANY)],
        out_specs=VMEM,
        out_shape=jax.ShapeDtypeStruct((seq_count, width), own.dtype),
        scratch_shapes=[
            pltpu.VMEM((seq_count, 16, width), own.dtype),
            pltpu.SemaphoreType.DMA((seq_count,)),
        ],
    )(lengths, own)


def last_rows_call(at, raw, gains):
    seq_count, width = raw[0].shape
    shape = (Z, 16, (Y - 1) * XLO * (width // (XLO * Z)))
    return pl.pallas_call(
        last_rows_kernel,
        in_specs=[SMEM] + [VMEM] * (len(raw) + 1),
        out_specs=VMEM,
        out_shape=jax.ShapeDtypeStruct(shape, jnp.bfloat16),
        scratch_shapes=[
            pltpu.VMEM((len(raw), seq_count, width), jnp.float32),
            pltpu.VMEM(shape, jnp.float32),
        ],
    )(at, *raw, gains)


def second_payload_call(z_all, rest):
    depth, width = rest[0].shape
    tail_rows = (width // HEAD_DIM - 1) * 8
    tail = z_all.shape[1] // 16 - 1
    return pl.pallas_call(
        second_payload_kernel,
        grid=(1,),
        in_specs=[pl.BlockSpec((Z, 16, z_all.shape[2]), lambda i: (0, tail, 0))]
        + [VMEM] * len(rest),
        out_specs=VMEM,
        out_shape=jax.ShapeDtypeStruct((Z, Y * depth + tail_rows + 16, HEAD_DIM), jnp.bfloat16),
        scratch_shapes=[pltpu.VMEM((Z, tail_rows, HEAD_DIM), jnp.float32)],
    )(z_all, *rest)


def kv_attend(at, lengths, slices, pieces, last, corner, gains, heads, qg, kg):
    seq_count, slots, width = slices[0].shape
    model_width = gains.size
    kv_width = 2 * HEAD_DIM
    rows = model_width // (Y * XLO * Z)
    per_step = 2
    x_spec = pl.BlockSpec((per_step, slots, width), lambda step: (step, 0, 0))
    return pl.pallas_call(
        kv_attend_kernel,
        grid=(seq_count // per_step,),
        in_specs=[SMEM, SMEM]
        + [x_spec] * len(slices)
        + [pl.BlockSpec(memory_space=pltpu.HBM)] * (len(pieces) + 2)
        + [VMEM] * 3,
        out_specs=pl.BlockSpec((per_step, heads, HEAD_DIM), lambda step: (step, 0, 0)),
        out_shape=jax.ShapeDtypeStruct((seq_count, heads, HEAD_DIM), jnp.float32),
        scratch_shapes=[pltpu.VMEM((Y, XLO, Z, rows, kv_width), jnp.bfloat16)] * 2
        + [
            pltpu.VMEM((Z, heads * 8, HEAD_DIM), jnp.bfloat16),
            pltpu.VMEM((heads * 8, HEAD_DIM), jnp.float32),
            pltpu.SemaphoreType.DMA((3,)),
        ],
        compiler_params=pltpu.CompilerParams(vmem_limit_bytes=58 * 1024 * 1024),
        cost_estimate=pl.CostEstimate(
            flops=4 * seq_count * slots * model_width * kv_width,
            bytes_accessed=2 * seq_count * slots * model_width + 4 * model_width * kv_width,
            transcendentals=seq_count * heads * slots,
        ),
    )(at, lengths, *slices, *pieces, last, corner, gains, qg, kg)


def body(
    hidden, lengths, norm_gain, q_norm_gain, k_norm_gain, query_weight, key_weight, value_weight
):
    tensor_size = lax.axis_size("tensor")
    tensor_at = lax.axis_index("tensor")
    dp_at = lax.axis_index("dp")
    x_lo_at = (dp_at >> (Z.bit_length() - 1)) & (XLO - 1)
    y_at = dp_at >> ((Z * XLO).bit_length() - 1)
    at = jnp.stack([y_at, x_lo_at, tensor_at]).astype(jnp.int32)

    pair_count, _, seq_slots, width_local = hidden.shape
    seq_count = 2 * pair_count
    own = hidden.reshape(seq_count, seq_slots, width_local)
    rows_local, kv_width = key_weight.shape
    query_width = query_weight.shape[1]
    gains = norm_gain[None]

    kv_weight = jnp.concatenate([key_weight, value_weight], axis=1)
    kv_both = jnp.concatenate([kv_weight, swap_x_lo(kv_weight)])
    query_other = swap_x_lo(query_weight)
    last_own = take_last_call(lengths, own)
    last_raw = [last_own] + [swap_tensor(last_own, k) for k in range(1, tensor_size)]

    sent_own = lax.optimization_barrier((own, kv_both, query_other, *last_raw))[0]
    far = swap_tensor(sent_own, 2)
    peer = swap_tensor(sent_own, 1)

    block = kv_both[:, : kv_width + HEAD_DIM]
    rows = last_rows_call(at, last_raw, gains)
    rows, _ = lax.optimization_barrier((rows, query_other))
    z_all = exchange(
        jnp.concatenate([jnp.broadcast_to(block[None], (Z,) + block.shape), rows], axis=1),
        Z_GROUPS,
    )

    rest = jnp.concatenate(
        [kv_both[:, kv_width + HEAD_DIM :], jnp.concatenate([query_weight, query_other])], axis=1
    )
    rest = [rest] + [shift(rest, dy=-step) for step in range(1, Y)]

    z_own = lax.optimization_barrier((z_all[:, : block.shape[0]], *rest))[0]
    z_up = shift(z_own, dy=-1)
    z_down = shift(z_own, dy=1)
    far_low = shift(z_up[: Z // 2], dy=-1)
    far_high = shift(z_down[Z // 2 :], dy=1)
    pieces = [z_own, z_up, z_down, far_low, far_high]

    corner = swap_tensor(z_own[0, :16], 1)
    second, corner = lax.optimization_barrier((second_payload_call(z_all, rest), corner))
    last = exchange(second, Z_GROUPS)
    far_peer = swap_tensor(lax.optimization_barrier((far, z_up, z_down))[0], 1)

    mixed = kv_attend(
        at,
        lengths,
        [own, peer, far, far_peer],
        pieces,
        last,
        corner,
        gains,
        query_width // HEAD_DIM,
        q_norm_gain[None],
        k_norm_gain[None],
    ).reshape(seq_count, width_local)

    sent = mixed.astype(jnp.bfloat16)
    every = exchange(jnp.broadcast_to(sent[None], (GROUPS * Z,) + sent.shape), None)
    every = every.reshape(-1, 2, width_local)
    dots = jnp.dot(every[:, 0], every[:, 1].T, preferred_element_type=jnp.float32)
    every_f32 = every.astype(jnp.float32)
    norms = jnp.sum(every_f32 * every_f32, axis=-1).T
    part = jnp.concatenate([dots, norms], axis=0)
    parts = [part] + [swap_tensor(part, k) for k in range(1, tensor_size)]
    total = (parts[0] + parts[1]) + (parts[2] + parts[3])
    pairs = dots.shape[0]
    scales = lax.rsqrt(total[pairs:] + EPS)
    sim = SCORE_SCALE * total[:pairs] * scales[0][:, None] * scales[1][None, :]
    row_lse = jax.nn.logsumexp(sim, axis=1)
    col_lse = jax.nn.logsumexp(sim, axis=0)
    positive = jnp.sum(jnp.where(jnp.eye(pairs, dtype=bool), sim, 0.0), axis=0)
    all_loss = 0.5 * (row_lse + col_lse) - positive
    loss = jnp.mean(all_loss)
    pair_loss = lax.dynamic_slice_in_dim(all_loss, dp_at * pair_count, pair_count)
    own_scale = lax.dynamic_slice_in_dim(scales, dp_at * pair_count, pair_count, axis=1)
    embeddings = (mixed.reshape(pair_count, 2, width_local) * own_scale.T[:, :, None]).astype(
        jnp.bfloat16
    )
    return (embeddings, pair_loss, loss)


def solution(mesh):
    in_specs = (
        P("dp", None, None, "tensor"),
        P("dp", None),
        P(),
        P(),
        P(),
        P("dp", "tensor"),
        P("dp", "tensor"),
        P("dp", "tensor"),
    )
    out_specs = (P("dp", None, "tensor"), P("dp"), P())
    return jax.shard_map(body, mesh=mesh, in_specs=in_specs, out_specs=out_specs, check_vma=False)
```

```python
import math

import jax
import jax.numpy as jnp
from jax import lax
from jax.experimental import pallas as pl
from jax.experimental.pallas import tpu as pltpu
from jax.sharding import PartitionSpec as P

HEAD_DIM = 128
EPS = 1e-06
SCORE_SCALE = 20.0

Y, XLO, Z = 4, 2, 8
XHI, CORES = 2, 2
GROUPS = Y * XLO
Z_GROUPS = [[g * Z + z for z in range(Z)] for g in range(GROUPS)]


def rms_rows(values):
    return values * lax.rsqrt(jnp.mean(values * values, axis=-1, keepdims=True) + EPS)


def shift(array, dx=0, dy=0, dz=0):
    pairs = []
    for y in range(Y):
        for x in range(XHI * XLO):
            for z in range(Z):
                for core in range(CORES):

                    def at(x, y, z):
                        x_hi, x_lo = divmod(x, XLO)
                        dp = (y * XLO + x_lo) * Z + z
                        return dp * (XHI * CORES) + x_hi * CORES + core

                    there = at((x + dx) % (XHI * XLO), (y + dy) % Y, (z + dz) % Z)
                    pairs.append((at(x, y, z), there))
    return lax.ppermute(array, ("dp", "tensor"), pairs)


def swap_tensor(array, mask):
    size = XHI * CORES
    return lax.ppermute(array, "tensor", [(i, i ^ mask) for i in range(size)])


def swap_x_lo(array):
    pairs = [(i, (i // Z ^ 1) * Z + i % Z) for i in range(GROUPS * Z)]
    return lax.ppermute(array, "dp", pairs)


def exchange(chunks, groups):
    return lax.all_to_all(
        chunks, "dp", split_axis=0, concat_axis=0, tiled=True, axis_index_groups=groups
    )


def take_last_kernel(len_ref, hidden_ref, out_ref, tile_ref, sem):
    seq_count, depth, width = tile_ref.shape
    spots = [len_ref[seq // 2, seq % 2] - 1 for seq in range(seq_count)]
    copies = []
    for seq, spot in enumerate(spots):
        rows = pl.ds(pl.multiple_of(spot & -depth, depth), depth)
        copies.append(
            pltpu.make_async_copy(hidden_ref.at[seq, rows, :], tile_ref.at[seq], sem.at[seq])
        )
        copies[-1].start()
    row_at = lax.broadcasted_iota(jnp.int32, (depth, width), 0)
    seq_at = lax.broadcasted_iota(jnp.int32, (seq_count, width), 0)
    rows = jnp.zeros((seq_count, width), jnp.float32)
    for seq, spot in enumerate(spots):
        copies[seq].wait()
        tile = tile_ref[seq].astype(jnp.float32)
        row = jnp.sum(jnp.where(row_at == (spot & (depth - 1)), tile, 0.0), axis=0, keepdims=True)
        rows = jnp.where(seq_at == seq, row, rows)
    out_ref[...] = rows.astype(jnp.bfloat16)


def last_rows_kernel(at_ref, r0, r1, r2, r3, gain_ref, out_ref, raw_ref, row_ref):
    y_at, x_lo_at, tensor_at = at_ref[0], at_ref[1], at_ref[2]
    refs = [r0, r1, r2, r3]
    seq_count, width = r0.shape
    rows = width // (XLO * Z)
    squares = None
    for k, ref in enumerate(refs):
        x = ref[...].astype(jnp.float32)
        raw_ref[k] = x
        part = jnp.sum(x * x, axis=-1, keepdims=True)
        squares = part if squares is None else squares + part
    scale = lax.rsqrt(squares / (len(refs) * width) + EPS)
    row_ref[...] = jnp.zeros_like(row_ref)
    for step in range(Y):
        slice_at = (y_at + step) & (Y - 1)
        normed = raw_ref[slice_at ^ tensor_at] * scale * gain_ref[
            :, pl.ds(pl.multiple_of(slice_at * width, width), width)
        ]
        normed = normed.astype(jnp.bfloat16).astype(jnp.float32)
        halves = [normed[:, : Z * rows], normed[:, Z * rows :]]
        row, lane = (0, step * XLO * rows) if step < Y - 1 else (8, 0)
        for x in range(XLO):
            half = jnp.where(x_lo_at == x, halves[0], halves[1])
            for z in range(Z):
                at = lane + x * rows
                row_ref[z, row : row + seq_count, at : at + rows] = half[
                    :, z * rows : (z + 1) * rows
                ]
    out_ref[...] = row_ref[...].astype(jnp.bfloat16)


def second_payload_kernel(rows_ref, w0, w1, w2, w3, out_ref, acc_ref):
    depth, _ = w0.shape
    rows = rows_ref[...].astype(jnp.float32)
    total = None
    for step, w_ref in enumerate([w0, w1, w2, w3]):
        row, lane = (0, step * depth) if step < Y - 1 else (8, 0)
        lhs = rows[:, row : row + 8, lane : lane + depth].reshape(Z * 8, depth)
        part = jnp.dot(
            lhs.astype(jnp.bfloat16), w_ref[:, HEAD_DIM:], preferred_element_type=jnp.float32
        )
        total = part if total is None else total + part
    high = total.astype(jnp.bfloat16).astype(jnp.float32)
    low = (total - high).astype(jnp.bfloat16).astype(jnp.float32)
    both = high + pltpu.roll(low, 4, 0)
    for head in range(both.shape[1] // HEAD_DIM):
        block = both[:, head * HEAD_DIM : (head + 1) * HEAD_DIM]
        acc_ref[:, head * 8 : (head + 1) * 8, :] = block.reshape(Z, 8, HEAD_DIM)
    for z in range(Z):
        for step, w_ref in enumerate([w0, w1, w2, w3]):
            out_ref[z, step * depth : (step + 1) * depth, :] = w_ref[:, :HEAD_DIM]
        tail = slice(Y * depth, Y * depth + acc_ref.shape[1])
        out_ref[z, tail, :] = acc_ref[z].astype(jnp.bfloat16)
        out_ref[z, tail.stop :, :] = jnp.zeros((16, HEAD_DIM), jnp.bfloat16)


def kv_attend_kernel(
    at_ref,
    len_ref,
    x0_ref,
    x1_ref,
    x2_ref,
    x3_ref,
    own_ref,
    up_ref,
    down_ref,
    far_low_ref,
    far_high_ref,
    last_ref,
    corner_ref,
    gain_ref,
    qg_ref,
    kg_ref,
    out_ref,
    wk_ref,
    wv_ref,
    parts_ref,
    query_ref,
    normed_ref,
    sem,
):
    del corner_ref
    x_refs = [x0_ref, x1_ref, x2_ref, x3_ref]
    per_step, slots, width = x0_ref.shape
    slices = len(x_refs)
    rows = width // (XLO * Z)
    step_at = pl.program_id(0)
    heads = out_ref.shape[1]
    y_at, x_lo_at, tensor_at = at_ref[0], at_ref[1], at_ref[2]

    @pl.when(step_at == 0)
    def _():
        low = Z // 2

        def start(source, target, at):
            pltpu.make_async_copy(source, target, sem.at[at]).start()

        sources = [[own_ref], [up_ref], [far_low_ref, far_high_ref], [down_ref]]
        for values in range(2):
            for step, halves in enumerate(sources):
                y = (y_at + step) & (Y - 1)
                for x in range(XLO):
                    block = pl.ds(x * rows, rows)
                    for half, piece in enumerate(halves):
                        zs = pl.ds(half * low, piece.shape[0])
                        if values:
                            columns = pl.ds(2 * HEAD_DIM, HEAD_DIM)
                            target = wv_ref.at[y, x_lo_at ^ x, zs, :, pl.ds(0, HEAD_DIM)]
                        else:
                            columns = pl.ds(0, 2 * HEAD_DIM)
                            target = wk_ref.at[y, x_lo_at ^ x, zs]
                        start(piece.at[:, block, columns], target, values)
                    if values:
                        block = pl.ds((step * XLO + x) * rows, rows)
                        target = wv_ref.at[y, x_lo_at ^ x, :, :, pl.ds(HEAD_DIM, HEAD_DIM)]
                        start(last_ref.at[:, block, :], target, values)
        start(last_ref.at[:, pl.ds(Y * XLO * rows, parts_ref.shape[1]), :], parts_ref, 2)

    squares = None
    for k in range(slices):
        x = x_refs[k][...].reshape(-1, width).astype(jnp.float32)
        part = jnp.sum(x * x, axis=-1, keepdims=True)
        squares = part if squares is None else squares + part
    scale = lax.rsqrt(squares / (slices * width) + EPS)

    @pl.when(step_at == 0)
    def _():
        pltpu.make_async_copy(wk_ref, wk_ref, sem.at[0]).wait()

    key_proj = value_proj = None
    for k in range(slices):
        x = x_refs[k][...].reshape(-1, width).astype(jnp.float32)
        slice_at = tensor_at ^ k
        at = pl.ds(pl.multiple_of(slice_at * width, width), width)
        normed = (x * scale * gain_ref[:, at]).astype(jnp.bfloat16)
        normed_ref[k] = normed
        wk = wk_ref[slice_at].reshape(width, -1)
        part = jnp.dot(normed, wk, preferred_element_type=jnp.float32)
        key_proj = part if key_proj is None else key_proj + part

    @pl.when(step_at == 0)
    def _():
        pltpu.make_async_copy(wv_ref, wv_ref, sem.at[1]).wait()
        pltpu.make_async_copy(parts_ref, parts_ref, sem.at[2]).wait()
        parts = jnp.sum(parts_ref[...].astype(jnp.float32), axis=0)
        query_ref[...] = parts + pltpu.roll(parts, parts.shape[0] - 4, 0)

    for k in range(slices):
        wv = wv_ref[tensor_at ^ k].reshape(width, -1)
        part = jnp.dot(normed_ref[k], wv, preferred_element_type=jnp.float32)
        value_proj = part if value_proj is None else value_proj + part
    first = lax.broadcasted_iota(jnp.int32, (heads, 1), 0) < heads // 2
    positions = lax.broadcasted_iota(jnp.int32, (1, slots), 1)
    keys = []
    for h in range(2):
        key = key_proj[:, h * HEAD_DIM : (h + 1) * HEAD_DIM]
        keys.append((rms_rows(key) * kg_ref[...]).astype(jnp.bfloat16))
    value = value_proj.astype(jnp.bfloat16)
    for j in range(per_step):
        seq = step_at * per_step + j
        own = slice(j * slots, (j + 1) * slots)
        query = query_ref[pl.ds(seq, heads, stride=8), :]
        query = (rms_rows(query) * qg_ref[...]).astype(jnp.bfloat16)
        scores = [
            lax.dot_general(
                query, key[own], (((1,), (1,)), ((), ())), preferred_element_type=jnp.float32
            )
            for key in keys
        ]
        scores = jnp.where(first, scores[0], scores[1]) / math.sqrt(HEAD_DIM)
        scores = jnp.where(positions < len_ref[seq >> 1, seq & 1], scores, -1e30)
        expo = jnp.exp(scores - jnp.max(scores, axis=-1, keepdims=True))
        weights = (expo / jnp.sum(expo, axis=-1, keepdims=True)).astype(jnp.bfloat16)
        mixed = jnp.dot(weights, value[own], preferred_element_type=jnp.float32)
        out_ref[j] = jnp.where(first, mixed[:, :HEAD_DIM], mixed[:, HEAD_DIM:])


SMEM = pl.BlockSpec(memory_space=pltpu.SMEM)
VMEM = pl.BlockSpec(memory_space=pltpu.VMEM)


def take_last_call(lengths, own):
    seq_count, _, width = own.shape
    return pl.pallas_call(
        take_last_kernel,
        in_specs=[SMEM, pl.BlockSpec(memory_space=pl.ANY)],
        out_specs=VMEM,
        out_shape=jax.ShapeDtypeStruct((seq_count, width), own.dtype),
        scratch_shapes=[
            pltpu.VMEM((seq_count, 16, width), own.dtype),
            pltpu.SemaphoreType.DMA((seq_count,)),
        ],
    )(lengths, own)


def last_rows_call(at, raw, gains):
    seq_count, width = raw[0].shape
    shape = (Z, 16, (Y - 1) * XLO * (width // (XLO * Z)))
    return pl.pallas_call(
        last_rows_kernel,
        in_specs=[SMEM] + [VMEM] * (len(raw) + 1),
        out_specs=VMEM,
        out_shape=jax.ShapeDtypeStruct(shape, jnp.bfloat16),
        scratch_shapes=[
            pltpu.VMEM((len(raw), seq_count, width), jnp.float32),
            pltpu.VMEM(shape, jnp.float32),
        ],
    )(at, *raw, gains)


def second_payload_call(z_all, rest):
    depth, width = rest[0].shape
    tail_rows = (width // HEAD_DIM - 1) * 8
    tail = z_all.shape[1] // 16 - 1
    return pl.pallas_call(
        second_payload_kernel,
        grid=(1,),
        in_specs=[pl.BlockSpec((Z, 16, z_all.shape[2]), lambda i: (0, tail, 0))]
        + [VMEM] * len(rest),
        out_specs=VMEM,
        out_shape=jax.ShapeDtypeStruct((Z, Y * depth + tail_rows + 16, HEAD_DIM), jnp.bfloat16),
        scratch_shapes=[pltpu.VMEM((Z, tail_rows, HEAD_DIM), jnp.float32)],
    )(z_all, *rest)


def kv_attend(at, lengths, slices, pieces, last, corner, gains, heads, qg, kg):
    seq_count, slots, width = slices[0].shape
    model_width = gains.size
    kv_width = 2 * HEAD_DIM
    rows = model_width // (Y * XLO * Z)
    per_step = 2
    x_spec = pl.BlockSpec((per_step, slots, width), lambda step: (step, 0, 0))
    return pl.pallas_call(
        kv_attend_kernel,
        grid=(seq_count // per_step,),
        in_specs=[SMEM, SMEM]
        + [x_spec] * len(slices)
        + [pl.BlockSpec(memory_space=pltpu.HBM)] * (len(pieces) + 2)
        + [VMEM] * 3,
        out_specs=pl.BlockSpec((per_step, heads, HEAD_DIM), lambda step: (step, 0, 0)),
        out_shape=jax.ShapeDtypeStruct((seq_count, heads, HEAD_DIM), jnp.float32),
        scratch_shapes=[pltpu.VMEM((Y, XLO, Z, rows, kv_width), jnp.bfloat16)] * 2
        + [
            pltpu.VMEM((Z, heads * 8, HEAD_DIM), jnp.bfloat16),
            pltpu.VMEM((heads * 8, HEAD_DIM), jnp.float32),
            pltpu.VMEM((len(slices), per_step * slots, width), jnp.bfloat16),
            pltpu.SemaphoreType.DMA((3,)),
        ],
        compiler_params=pltpu.CompilerParams(vmem_limit_bytes=58 * 1024 * 1024),
        cost_estimate=pl.CostEstimate(
            flops=4 * seq_count * slots * model_width * kv_width,
            bytes_accessed=2 * seq_count * slots * model_width + 4 * model_width * kv_width,
            transcendentals=seq_count * heads * slots,
        ),
    )(at, lengths, *slices, *pieces, last, corner, gains, qg, kg)


def body(
    hidden, lengths, norm_gain, q_norm_gain, k_norm_gain, query_weight, key_weight, value_weight
):
    tensor_size = lax.axis_size("tensor")
    tensor_at = lax.axis_index("tensor")
    dp_at = lax.axis_index("dp")
    x_lo_at = (dp_at >> (Z.bit_length() - 1)) & (XLO - 1)
    y_at = dp_at >> ((Z * XLO).bit_length() - 1)
    at = jnp.stack([y_at, x_lo_at, tensor_at]).astype(jnp.int32)

    pair_count, _, seq_slots, width_local = hidden.shape
    seq_count = 2 * pair_count
    own = hidden.reshape(seq_count, seq_slots, width_local)
    rows_local, kv_width = key_weight.shape
    query_width = query_weight.shape[1]
    gains = norm_gain[None]

    kv_weight = jnp.concatenate([key_weight, value_weight], axis=1)
    kv_both = jnp.concatenate([kv_weight, swap_x_lo(kv_weight)])
    query_other = swap_x_lo(query_weight)
    last_own = take_last_call(lengths, own)
    last_raw = [last_own] + [swap_tensor(last_own, k) for k in range(1, tensor_size)]

    sent_own = lax.optimization_barrier((own, kv_both, query_other, *last_raw))[0]
    far = swap_tensor(sent_own, 2)
    peer = swap_tensor(sent_own, 1)

    block = kv_both[:, : kv_width + HEAD_DIM]
    rows = last_rows_call(at, last_raw, gains)
    payload = jnp.concatenate([jnp.broadcast_to(block[None], (Z,) + block.shape), rows], axis=1)
    payload, _ = lax.optimization_barrier((payload, query_other))
    z_all = exchange(payload, Z_GROUPS)

    rest = jnp.concatenate(
        [kv_both[:, kv_width + HEAD_DIM :], jnp.concatenate([query_weight, query_other])], axis=1
    )
    rest = [rest] + [shift(rest, dy=-step) for step in range(1, Y)]

    z_own = lax.optimization_barrier((z_all[:, : block.shape[0]], *rest))[0]
    z_up = shift(z_own, dy=-1)
    z_down = shift(z_own, dy=1)
    far_low = shift(z_up[: Z // 2], dy=-1)
    far_high = shift(z_down[Z // 2 :], dy=1)
    pieces = [z_own, z_up, z_down, far_low, far_high]

    corner = swap_tensor(z_own[0, :16], 1)
    second, corner = lax.optimization_barrier((second_payload_call(z_all, rest), corner))
    last = exchange(second, Z_GROUPS)
    far_peer = swap_tensor(lax.optimization_barrier((far, z_up, z_down))[0], 1)

    mixed = kv_attend(
        at,
        lengths,
        [own, peer, far, far_peer],
        pieces,
        last,
        corner,
        gains,
        query_width // HEAD_DIM,
        q_norm_gain[None],
        k_norm_gain[None],
    ).reshape(seq_count, width_local)

    sent = mixed.astype(jnp.bfloat16)
    every = exchange(jnp.broadcast_to(sent[None], (GROUPS * Z,) + sent.shape), None)
    every = every.reshape(-1, 2, width_local)
    dots = jnp.dot(every[:, 0], every[:, 1].T, preferred_element_type=jnp.float32)
    every_f32 = every.astype(jnp.float32)
    norms = jnp.sum(every_f32 * every_f32, axis=-1).T
    part = jnp.concatenate([dots, norms], axis=0)
    parts = [part] + [swap_tensor(part, k) for k in range(1, tensor_size)]
    total = (parts[0] + parts[1]) + (parts[2] + parts[3])
    pairs = dots.shape[0]
    scales = lax.rsqrt(total[pairs:] + EPS)
    sim = SCORE_SCALE * total[:pairs] * scales[0][:, None] * scales[1][None, :]
    row_lse = jax.nn.logsumexp(sim, axis=1)
    col_lse = jax.nn.logsumexp(sim, axis=0)
    positive = jnp.sum(jnp.where(jnp.eye(pairs, dtype=bool), sim, 0.0), axis=0)
    all_loss = 0.5 * (row_lse + col_lse) - positive
    loss = jnp.mean(all_loss)
    pair_loss = lax.dynamic_slice_in_dim(all_loss, dp_at * pair_count, pair_count)
    own_scale = lax.dynamic_slice_in_dim(scales, dp_at * pair_count, pair_count, axis=1)
    embeddings = (mixed.reshape(pair_count, 2, width_local) * own_scale.T[:, :, None]).astype(
        jnp.bfloat16
    )
    return (embeddings, pair_loss, loss)


def solution(mesh):
    in_specs = (
        P("dp", None, None, "tensor"),
        P("dp", None),
        P(),
        P(),
        P(),
        P("dp", "tensor"),
        P("dp", "tensor"),
        P("dp", "tensor"),
    )
    out_specs = (P("dp", None, "tensor"), P("dp"), P())
    return jax.shard_map(body, mesh=mesh, in_specs=in_specs, out_specs=out_specs, check_vma=False)
```

```python
import math

import jax
import jax.numpy as jnp
from jax import lax
from jax.experimental import pallas as pl
from jax.experimental.pallas import tpu as pltpu
from jax.sharding import PartitionSpec as P

HEAD_DIM = 128
EPS = 1e-06
SCORE_SCALE = 20.0

Y, XLO, Z = 4, 2, 8
XHI, CORES = 2, 2
GROUPS = Y * XLO
Z_GROUPS = [[g * Z + z for z in range(Z)] for g in range(GROUPS)]


def rms_rows(values):
    return values * lax.rsqrt(jnp.mean(values * values, axis=-1, keepdims=True) + EPS)


def shift(array, dx=0, dy=0, dz=0):
    pairs = []
    for y in range(Y):
        for x in range(XHI * XLO):
            for z in range(Z):
                for core in range(CORES):

                    def at(x, y, z):
                        x_hi, x_lo = divmod(x, XLO)
                        dp = (y * XLO + x_lo) * Z + z
                        return dp * (XHI * CORES) + x_hi * CORES + core

                    there = at((x + dx) % (XHI * XLO), (y + dy) % Y, (z + dz) % Z)
                    pairs.append((at(x, y, z), there))
    return lax.ppermute(array, ("dp", "tensor"), pairs)


def swap_tensor(array, mask):
    size = XHI * CORES
    return lax.ppermute(array, "tensor", [(i, i ^ mask) for i in range(size)])


def swap_x_lo(array):
    pairs = [(i, (i // Z ^ 1) * Z + i % Z) for i in range(GROUPS * Z)]
    return lax.ppermute(array, "dp", pairs)


def exchange(chunks, groups):
    return lax.all_to_all(
        chunks, "dp", split_axis=0, concat_axis=0, tiled=True, axis_index_groups=groups
    )


def take_last_kernel(len_ref, hidden_ref, out_ref, tile_ref, sem):
    seq_count, depth, width = tile_ref.shape
    spots = [len_ref[seq // 2, seq % 2] - 1 for seq in range(seq_count)]
    copies = []
    for seq, spot in enumerate(spots):
        rows = pl.ds(pl.multiple_of(spot & -depth, depth), depth)
        copies.append(
            pltpu.make_async_copy(hidden_ref.at[seq, rows, :], tile_ref.at[seq], sem.at[seq])
        )
        copies[-1].start()
    row_at = lax.broadcasted_iota(jnp.int32, (depth, width), 0)
    seq_at = lax.broadcasted_iota(jnp.int32, (seq_count, width), 0)
    rows = jnp.zeros((seq_count, width), jnp.float32)
    for seq, spot in enumerate(spots):
        copies[seq].wait()
        tile = tile_ref[seq].astype(jnp.float32)
        row = jnp.sum(jnp.where(row_at == (spot & (depth - 1)), tile, 0.0), axis=0, keepdims=True)
        rows = jnp.where(seq_at == seq, row, rows)
    out_ref[...] = rows.astype(jnp.bfloat16)


def last_rows_kernel(at_ref, r0, r1, r2, r3, gain_ref, out_ref, raw_ref, row_ref):
    y_at, x_lo_at, tensor_at = at_ref[0], at_ref[1], at_ref[2]
    refs = [r0, r1, r2, r3]
    seq_count, width = r0.shape
    rows = width // (XLO * Z)
    squares = None
    for k, ref in enumerate(refs):
        x = ref[...].astype(jnp.float32)
        raw_ref[k] = x
        part = jnp.sum(x * x, axis=-1, keepdims=True)
        squares = part if squares is None else squares + part
    scale = lax.rsqrt(squares / (len(refs) * width) + EPS)
    row_ref[...] = jnp.zeros_like(row_ref)
    for step in range(Y):
        slice_at = (y_at + step) & (Y - 1)
        normed = raw_ref[slice_at ^ tensor_at] * scale * gain_ref[
            :, pl.ds(pl.multiple_of(slice_at * width, width), width)
        ]
        normed = normed.astype(jnp.bfloat16).astype(jnp.float32)
        halves = [normed[:, : Z * rows], normed[:, Z * rows :]]
        row, lane = (0, step * XLO * rows) if step < Y - 1 else (8, 0)
        for x in range(XLO):
            half = jnp.where(x_lo_at == x, halves[0], halves[1])
            for z in range(Z):
                at = lane + x * rows
                row_ref[z, row : row + seq_count, at : at + rows] = half[
                    :, z * rows : (z + 1) * rows
                ]
    out_ref[...] = row_ref[...].astype(jnp.bfloat16)


def second_payload_kernel(rows_ref, w0, w1, w2, w3, out_ref, acc_ref):
    depth, _ = w0.shape
    rows = rows_ref[...].astype(jnp.float32)
    total = None
    for step, w_ref in enumerate([w0, w1, w2, w3]):
        row, lane = (0, step * depth) if step < Y - 1 else (8, 0)
        lhs = rows[:, row : row + 8, lane : lane + depth].reshape(Z * 8, depth)
        part = jnp.dot(
            lhs.astype(jnp.bfloat16), w_ref[:, HEAD_DIM:], preferred_element_type=jnp.float32
        )
        total = part if total is None else total + part
    high = total.astype(jnp.bfloat16).astype(jnp.float32)
    low = (total - high).astype(jnp.bfloat16).astype(jnp.float32)
    both = high + pltpu.roll(low, 4, 0)
    for head in range(both.shape[1] // HEAD_DIM):
        block = both[:, head * HEAD_DIM : (head + 1) * HEAD_DIM]
        acc_ref[:, head * 8 : (head + 1) * 8, :] = block.reshape(Z, 8, HEAD_DIM)
    for z in range(Z):
        for step, w_ref in enumerate([w0, w1, w2, w3]):
            out_ref[z, step * depth : (step + 1) * depth, :] = w_ref[:, :HEAD_DIM]
        tail = slice(Y * depth, Y * depth + acc_ref.shape[1])
        out_ref[z, tail, :] = acc_ref[z].astype(jnp.bfloat16)
        out_ref[z, tail.stop :, :] = jnp.zeros((16, HEAD_DIM), jnp.bfloat16)


def kv_attend_kernel(
    at_ref,
    len_ref,
    x0_ref,
    x1_ref,
    x2_ref,
    x3_ref,
    own_ref,
    up_ref,
    down_ref,
    far_low_ref,
    far_high_ref,
    last_ref,
    corner_ref,
    gain_ref,
    qg_ref,
    kg_ref,
    out_ref,
    wk_ref,
    wv_ref,
    parts_ref,
    query_ref,
    sem,
):
    del corner_ref
    x_refs = [x0_ref, x1_ref, x2_ref, x3_ref]
    per_step, slots, width = x0_ref.shape
    slices = len(x_refs)
    rows = width // (XLO * Z)
    step_at = pl.program_id(0)
    heads = out_ref.shape[1]
    y_at, x_lo_at, tensor_at = at_ref[0], at_ref[1], at_ref[2]

    @pl.when(step_at == 0)
    def _():
        low = Z // 2

        def start(source, target, at):
            pltpu.make_async_copy(source, target, sem.at[at]).start()

        start(last_ref.at[:, pl.ds(Y * XLO * rows, parts_ref.shape[1]), :], parts_ref, 2)
        for step, halves in enumerate(
            [[own_ref], [up_ref], [far_low_ref, far_high_ref], [down_ref]]
        ):
            y = (y_at + step) & (Y - 1)
            for x in range(XLO):
                block = pl.ds(x * rows, rows)
                for half, piece in enumerate(halves):
                    zs = pl.ds(half * low, piece.shape[0])
                    wk_at = wk_ref.at[y, x_lo_at ^ x, zs]
                    start(piece.at[:, block, pl.ds(0, 2 * HEAD_DIM)], wk_at, 0)
                    wv_at = wv_ref.at[y, x_lo_at ^ x, zs, :, pl.ds(0, HEAD_DIM)]
                    start(piece.at[:, block, pl.ds(2 * HEAD_DIM, HEAD_DIM)], wv_at, 1)
                block = pl.ds((step * XLO + x) * rows, rows)
                wv_at = wv_ref.at[y, x_lo_at ^ x, :, :, pl.ds(HEAD_DIM, HEAD_DIM)]
                start(last_ref.at[:, block, :], wv_at, 1)

    squares = None
    for k in range(slices):
        x = x_refs[k][...].reshape(-1, width).astype(jnp.float32)
        part = jnp.sum(x * x, axis=-1, keepdims=True)
        squares = part if squares is None else squares + part
    scale = lax.rsqrt(squares / (slices * width) + EPS)

    @pl.when(step_at == 0)
    def _():
        for at, ref in enumerate([wk_ref, wv_ref, parts_ref]):
            pltpu.make_async_copy(ref, ref, sem.at[at]).wait()
        parts = jnp.sum(parts_ref[...].astype(jnp.float32), axis=0)
        query_ref[...] = parts + pltpu.roll(parts, parts.shape[0] - 4, 0)

    key_proj = value_proj = None
    for k in range(slices):
        x = x_refs[k][...].reshape(-1, width).astype(jnp.float32)
        slice_at = tensor_at ^ k
        at = pl.ds(pl.multiple_of(slice_at * width, width), width)
        normed = (x * scale * gain_ref[:, at]).astype(jnp.bfloat16)
        wk = wk_ref[slice_at].reshape(width, -1)
        wv = wv_ref[slice_at].reshape(width, -1)
        kp = jnp.dot(normed, wk, preferred_element_type=jnp.float32)
        vp = jnp.dot(normed, wv, preferred_element_type=jnp.float32)
        key_proj = kp if key_proj is None else key_proj + kp
        value_proj = vp if value_proj is None else value_proj + vp
    first = lax.broadcasted_iota(jnp.int32, (heads, 1), 0) < heads // 2
    positions = lax.broadcasted_iota(jnp.int32, (1, slots), 1)
    keys = []
    for h in range(2):
        key = key_proj[:, h * HEAD_DIM : (h + 1) * HEAD_DIM]
        keys.append((rms_rows(key) * kg_ref[...]).astype(jnp.bfloat16))
    value = value_proj.astype(jnp.bfloat16)
    for j in range(per_step):
        seq = step_at * per_step + j
        own = slice(j * slots, (j + 1) * slots)
        query = query_ref[pl.ds(seq, heads, stride=8), :]
        query = (rms_rows(query) * qg_ref[...]).astype(jnp.bfloat16)
        scores = [
            lax.dot_general(
                query, key[own], (((1,), (1,)), ((), ())), preferred_element_type=jnp.float32
            )
            for key in keys
        ]
        scores = jnp.where(first, scores[0], scores[1]) / math.sqrt(HEAD_DIM)
        scores = jnp.where(positions < len_ref[seq >> 1, seq & 1], scores, -1e30)
        expo = jnp.exp(scores - jnp.max(scores, axis=-1, keepdims=True))
        weights = (expo / jnp.sum(expo, axis=-1, keepdims=True)).astype(jnp.bfloat16)
        mixed = jnp.dot(weights, value[own], preferred_element_type=jnp.float32)
        out_ref[j] = jnp.where(first, mixed[:, :HEAD_DIM], mixed[:, HEAD_DIM:])


SMEM = pl.BlockSpec(memory_space=pltpu.SMEM)
VMEM = pl.BlockSpec(memory_space=pltpu.VMEM)


def take_last_call(lengths, own):
    seq_count, _, width = own.shape
    return pl.pallas_call(
        take_last_kernel,
        in_specs=[SMEM, pl.BlockSpec(memory_space=pl.ANY)],
        out_specs=VMEM,
        out_shape=jax.ShapeDtypeStruct((seq_count, width), own.dtype),
        scratch_shapes=[
            pltpu.VMEM((seq_count, 16, width), own.dtype),
            pltpu.SemaphoreType.DMA((seq_count,)),
        ],
    )(lengths, own)


def last_rows_call(at, raw, gains):
    seq_count, width = raw[0].shape
    shape = (Z, 16, (Y - 1) * XLO * (width // (XLO * Z)))
    return pl.pallas_call(
        last_rows_kernel,
        in_specs=[SMEM] + [VMEM] * (len(raw) + 1),
        out_specs=VMEM,
        out_shape=jax.ShapeDtypeStruct(shape, jnp.bfloat16),
        scratch_shapes=[
            pltpu.VMEM((len(raw), seq_count, width), jnp.float32),
            pltpu.VMEM(shape, jnp.float32),
        ],
    )(at, *raw, gains)


def second_payload_call(z_all, rest):
    depth, width = rest[0].shape
    tail_rows = (width // HEAD_DIM - 1) * 8
    tail = z_all.shape[1] // 16 - 1
    return pl.pallas_call(
        second_payload_kernel,
        grid=(1,),
        in_specs=[pl.BlockSpec((Z, 16, z_all.shape[2]), lambda i: (0, tail, 0))]
        + [VMEM] * len(rest),
        out_specs=VMEM,
        out_shape=jax.ShapeDtypeStruct((Z, Y * depth + tail_rows + 16, HEAD_DIM), jnp.bfloat16),
        scratch_shapes=[pltpu.VMEM((Z, tail_rows, HEAD_DIM), jnp.float32)],
    )(z_all, *rest)


def kv_attend(at, lengths, slices, pieces, last, corner, gains, heads, qg, kg):
    seq_count, slots, width = slices[0].shape
    model_width = gains.size
    kv_width = 2 * HEAD_DIM
    rows = model_width // (Y * XLO * Z)
    per_step = 2
    x_spec = pl.BlockSpec((per_step, slots, width), lambda step: (step, 0, 0))
    return pl.pallas_call(
        kv_attend_kernel,
        grid=(seq_count // per_step,),
        in_specs=[SMEM, SMEM]
        + [x_spec] * len(slices)
        + [pl.BlockSpec(memory_space=pltpu.HBM)] * (len(pieces) + 2)
        + [VMEM] * 3,
        out_specs=pl.BlockSpec((per_step, heads, HEAD_DIM), lambda step: (step, 0, 0)),
        out_shape=jax.ShapeDtypeStruct((seq_count, heads, HEAD_DIM), jnp.float32),
        scratch_shapes=[pltpu.VMEM((Y, XLO, Z, rows, kv_width), jnp.bfloat16)] * 2
        + [
            pltpu.VMEM((Z, heads * 8, HEAD_DIM), jnp.bfloat16),
            pltpu.VMEM((heads * 8, HEAD_DIM), jnp.float32),
            pltpu.SemaphoreType.DMA((3,)),
        ],
        compiler_params=pltpu.CompilerParams(vmem_limit_bytes=58 * 1024 * 1024),
        cost_estimate=pl.CostEstimate(
            flops=4 * seq_count * slots * model_width * kv_width,
            bytes_accessed=2 * seq_count * slots * model_width + 4 * model_width * kv_width,
            transcendentals=seq_count * heads * slots,
        ),
    )(at, lengths, *slices, *pieces, last, corner, gains, qg, kg)


def body(
    hidden, lengths, norm_gain, q_norm_gain, k_norm_gain, query_weight, key_weight, value_weight
):
    tensor_size = lax.axis_size("tensor")
    tensor_at = lax.axis_index("tensor")
    dp_at = lax.axis_index("dp")
    x_lo_at = (dp_at >> (Z.bit_length() - 1)) & (XLO - 1)
    y_at = dp_at >> ((Z * XLO).bit_length() - 1)
    at = jnp.stack([y_at, x_lo_at, tensor_at]).astype(jnp.int32)

    pair_count, _, seq_slots, width_local = hidden.shape
    seq_count = 2 * pair_count
    own = hidden.reshape(seq_count, seq_slots, width_local)
    rows_local, kv_width = key_weight.shape
    query_width = query_weight.shape[1]
    gains = norm_gain[None]

    kv_weight = jnp.concatenate([key_weight, value_weight], axis=1)
    kv_both = jnp.concatenate([kv_weight, swap_x_lo(kv_weight)])
    query_other = swap_x_lo(query_weight)
    last_own = take_last_call(lengths, own)
    last_raw = [last_own] + [swap_tensor(last_own, k) for k in range(1, tensor_size)]

    sent_own = lax.optimization_barrier((own, kv_both, query_other, *last_raw))[0]
    far = swap_tensor(sent_own, 2)
    peer = swap_tensor(sent_own, 1)

    block = kv_both[:, : kv_width + HEAD_DIM]
    rows = last_rows_call(at, last_raw, gains)
    rows, _ = lax.optimization_barrier((rows, query_other))
    z_all = exchange(
        jnp.concatenate([jnp.broadcast_to(block[None], (Z,) + block.shape), rows], axis=1),
        Z_GROUPS,
    )

    rest = jnp.concatenate(
        [kv_both[:, kv_width + HEAD_DIM :], jnp.concatenate([query_weight, query_other])], axis=1
    )
    rest = [rest] + [shift(rest, dy=-step) for step in range(1, Y)]

    z_own = lax.optimization_barrier((z_all, *rest))[0]
    z_up = shift(z_own, dy=-1)
    z_down = shift(z_own, dy=1)
    far_low = shift(z_up[: Z // 2], dy=-1)
    far_high = shift(z_down[Z // 2 :], dy=1)
    pieces = [z_own, z_up, z_down, far_low, far_high]

    corner = swap_tensor(z_own[0, :16], 1)
    second, corner = lax.optimization_barrier((second_payload_call(z_all, rest), corner))
    last = exchange(second, Z_GROUPS)
    far_peer = swap_tensor(lax.optimization_barrier((far, z_up, z_down))[0], 1)

    mixed = kv_attend(
        at,
        lengths,
        [own, peer, far, far_peer],
        pieces,
        last,
        corner,
        gains,
        query_width // HEAD_DIM,
        q_norm_gain[None],
        k_norm_gain[None],
    ).reshape(seq_count, width_local)

    sent = mixed.astype(jnp.bfloat16)
    every = exchange(jnp.broadcast_to(sent[None], (GROUPS * Z,) + sent.shape), None)
    every = every.reshape(-1, 2, width_local)
    dots = jnp.dot(every[:, 0], every[:, 1].T, preferred_element_type=jnp.float32)
    every_f32 = every.astype(jnp.float32)
    norms = jnp.sum(every_f32 * every_f32, axis=-1).T
    part = jnp.concatenate([dots, norms], axis=0)
    parts = [part] + [swap_tensor(part, k) for k in range(1, tensor_size)]
    total = (parts[0] + parts[1]) + (parts[2] + parts[3])
    pairs = dots.shape[0]
    scales = lax.rsqrt(total[pairs:] + EPS)
    sim = SCORE_SCALE * total[:pairs] * scales[0][:, None] * scales[1][None, :]
    row_lse = jax.nn.logsumexp(sim, axis=1)
    col_lse = jax.nn.logsumexp(sim, axis=0)
    positive = jnp.sum(jnp.where(jnp.eye(pairs, dtype=bool), sim, 0.0), axis=0)
    all_loss = 0.5 * (row_lse + col_lse) - positive
    loss = jnp.mean(all_loss)
    pair_loss = lax.dynamic_slice_in_dim(all_loss, dp_at * pair_count, pair_count)
    own_scale = lax.dynamic_slice_in_dim(scales, dp_at * pair_count, pair_count, axis=1)
    embeddings = (mixed.reshape(pair_count, 2, width_local) * own_scale.T[:, :, None]).astype(
        jnp.bfloat16
    )
    return (embeddings, pair_loss, loss)


def solution(mesh):
    in_specs = (
        P("dp", None, None, "tensor"),
        P("dp", None),
        P(),
        P(),
        P(),
        P("dp", "tensor"),
        P("dp", "tensor"),
        P("dp", "tensor"),
    )
    out_specs = (P("dp", None, "tensor"), P("dp"), P())
    return jax.shard_map(body, mesh=mesh, in_specs=in_specs, out_specs=out_specs, check_vma=False)
```

```python
import math

import jax
import jax.numpy as jnp
from jax import lax
from jax.experimental import pallas as pl
from jax.experimental.pallas import tpu as pltpu
from jax.sharding import PartitionSpec as P

HEAD_DIM = 128
EPS = 1e-06
SCORE_SCALE = 20.0

Y, XLO, Z = 4, 2, 8
XHI, CORES = 2, 2
GROUPS = Y * XLO
XZ_GROUPS = [[y * XLO * Z + i for i in range(XLO * Z)] for y in range(Y)]
Y_GROUPS = [[y * XLO * Z + i for y in range(Y)] for i in range(XLO * Z)]
Z_GROUPS = [[g * Z + z for z in range(Z)] for g in range(GROUPS)]


def rms_rows(values):
    return values * lax.rsqrt(jnp.mean(values * values, axis=-1, keepdims=True) + EPS)


def shift(array, dx=0, dy=0, dz=0):
    pairs = []
    for y in range(Y):
        for x in range(XHI * XLO):
            for z in range(Z):
                for core in range(CORES):

                    def at(x, y, z):
                        x_hi, x_lo = divmod(x, XLO)
                        dp = (y * XLO + x_lo) * Z + z
                        return dp * (XHI * CORES) + x_hi * CORES + core

                    there = at((x + dx) % (XHI * XLO), (y + dy) % Y, (z + dz) % Z)
                    pairs.append((at(x, y, z), there))
    return lax.ppermute(array, ("dp", "tensor"), pairs)


def swap_tensor(array, mask):
    size = XHI * CORES
    return lax.ppermute(array, "tensor", [(i, i ^ mask) for i in range(size)])


def swap_x_lo(array):
    pairs = [(i, (i // Z ^ 1) * Z + i % Z) for i in range(GROUPS * Z)]
    return lax.ppermute(array, "dp", pairs)


def exchange(chunks, groups):
    return lax.all_to_all(
        chunks, "dp", split_axis=0, concat_axis=0, tiled=True, axis_index_groups=groups
    )


def take_last_kernel(len_ref, hidden_ref, out_ref, tile_ref, sem):
    seq_count, depth, width = tile_ref.shape
    spots = [len_ref[seq // 2, seq % 2] - 1 for seq in range(seq_count)]
    copies = []
    for seq, spot in enumerate(spots):
        rows = pl.ds(pl.multiple_of(spot & -depth, depth), depth)
        copies.append(
            pltpu.make_async_copy(hidden_ref.at[seq, rows, :], tile_ref.at[seq], sem.at[seq])
        )
        copies[-1].start()
    row_at = lax.broadcasted_iota(jnp.int32, (depth, width), 0)
    seq_at = lax.broadcasted_iota(jnp.int32, (seq_count, width), 0)
    rows = jnp.zeros((seq_count, width), jnp.float32)
    for seq, spot in enumerate(spots):
        copies[seq].wait()
        tile = tile_ref[seq].astype(jnp.float32)
        row = jnp.sum(jnp.where(row_at == (spot & (depth - 1)), tile, 0.0), axis=0, keepdims=True)
        rows = jnp.where(seq_at == seq, row, rows)
    out_ref[...] = rows.astype(jnp.bfloat16)


def last_rows_kernel(at_ref, r0, r1, r2, r3, gain_ref, out_ref, raw_ref, row_ref):
    y_at, x_lo_at, tensor_at = at_ref[0], at_ref[1], at_ref[2]
    refs = [r0, r1, r2, r3]
    seq_count, width = r0.shape
    rows = width // (XLO * Z)
    squares = None
    for k, ref in enumerate(refs):
        x = ref[...].astype(jnp.float32)
        raw_ref[k] = x
        part = jnp.sum(x * x, axis=-1, keepdims=True)
        squares = part if squares is None else squares + part
    scale = lax.rsqrt(squares / (len(refs) * width) + EPS)
    row_ref[...] = jnp.zeros_like(row_ref)
    for step in range(Y):
        slice_at = (y_at + step) & (Y - 1)
        normed = raw_ref[slice_at ^ tensor_at] * scale * gain_ref[
            :, pl.ds(pl.multiple_of(slice_at * width, width), width)
        ]
        normed = normed.astype(jnp.bfloat16).astype(jnp.float32)
        halves = [normed[:, : Z * rows], normed[:, Z * rows :]]
        row, lane = (0, step * XLO * rows) if step < Y - 1 else (8, 0)
        for x in range(XLO):
            half = jnp.where(x_lo_at == x, halves[0], halves[1])
            for z in range(Z):
                at = lane + x * rows
                row_ref[z, row : row + seq_count, at : at + rows] = half[
                    :, z * rows : (z + 1) * rows
                ]
    out_ref[...] = row_ref[...].astype(jnp.bfloat16)


def second_payload_kernel(rows_ref, w0, w1, w2, w3, out_ref, acc_ref):
    depth, _ = w0.shape
    rows = rows_ref[...].astype(jnp.float32)
    total = None
    for step, w_ref in enumerate([w0, w1, w2, w3]):
        row, lane = (0, step * depth) if step < Y - 1 else (8, 0)
        lhs = rows[:, row : row + 8, lane : lane + depth].reshape(Z * 8, depth)
        part = jnp.dot(
            lhs.astype(jnp.bfloat16), w_ref[:, HEAD_DIM:], preferred_element_type=jnp.float32
        )
        total = part if total is None else total + part
    high = total.astype(jnp.bfloat16).astype(jnp.float32)
    low = (total - high).astype(jnp.bfloat16).astype(jnp.float32)
    both = high + pltpu.roll(low, 4, 0)
    for head in range(both.shape[1] // HEAD_DIM):
        block = both[:, head * HEAD_DIM : (head + 1) * HEAD_DIM]
        acc_ref[:, head * 8 : (head + 1) * 8, :] = block.reshape(Z, 8, HEAD_DIM)
    for z in range(Z):
        for step, w_ref in enumerate([w0, w1, w2, w3]):
            out_ref[z, step * depth : (step + 1) * depth, :] = w_ref[:, :HEAD_DIM]
        tail = slice(Y * depth, Y * depth + acc_ref.shape[1])
        out_ref[z, tail, :] = acc_ref[z].astype(jnp.bfloat16)
        out_ref[z, tail.stop :, :] = jnp.zeros((16, HEAD_DIM), jnp.bfloat16)


def kv_attend_kernel(
    at_ref,
    len_ref,
    x0_ref,
    x1_ref,
    x2_ref,
    x3_ref,
    own_ref,
    up_ref,
    down_ref,
    far_low_ref,
    far_high_ref,
    last_ref,
    corner_ref,
    gain_ref,
    qg_ref,
    kg_ref,
    out_ref,
    wk_ref,
    wv_ref,
    parts_ref,
    query_ref,
    sem,
):
    del corner_ref
    x_refs = [x0_ref, x1_ref, x2_ref, x3_ref]
    per_step, slots, width = x0_ref.shape
    slices = len(x_refs)
    rows = width // (XLO * Z)
    step_at = pl.program_id(0)
    heads = out_ref.shape[1]
    y_at, x_lo_at, tensor_at = at_ref[0], at_ref[1], at_ref[2]

    @pl.when(step_at == 0)
    def _():
        low = Z // 2

        def start(source, target, at):
            pltpu.make_async_copy(source, target, sem.at[at]).start()

        start(last_ref.at[:, pl.ds(Y * XLO * rows, parts_ref.shape[1]), :], parts_ref, 2)
        for step, halves in enumerate(
            [[own_ref], [up_ref], [far_low_ref, far_high_ref], [down_ref]]
        ):
            y = (y_at + step) & (Y - 1)
            for x in range(XLO):
                block = pl.ds(x * rows, rows)
                for half, piece in enumerate(halves):
                    zs = pl.ds(half * low, piece.shape[0])
                    wk_at = wk_ref.at[y, x_lo_at ^ x, zs]
                    start(piece.at[:, block, pl.ds(0, 2 * HEAD_DIM)], wk_at, 0)
                    wv_at = wv_ref.at[y, x_lo_at ^ x, zs, :, pl.ds(0, HEAD_DIM)]
                    start(piece.at[:, block, pl.ds(2 * HEAD_DIM, HEAD_DIM)], wv_at, 1)
                block = pl.ds((step * XLO + x) * rows, rows)
                wv_at = wv_ref.at[y, x_lo_at ^ x, :, :, pl.ds(HEAD_DIM, HEAD_DIM)]
                start(last_ref.at[:, block, :], wv_at, 1)

    squares = None
    for k in range(slices):
        x = x_refs[k][...].reshape(-1, width).astype(jnp.float32)
        part = jnp.sum(x * x, axis=-1, keepdims=True)
        squares = part if squares is None else squares + part
    scale = lax.rsqrt(squares / (slices * width) + EPS)

    @pl.when(step_at == 0)
    def _():
        for at, ref in enumerate([wk_ref, wv_ref, parts_ref]):
            pltpu.make_async_copy(ref, ref, sem.at[at]).wait()
        parts = jnp.sum(parts_ref[...].astype(jnp.float32), axis=0)
        query_ref[...] = parts + pltpu.roll(parts, parts.shape[0] - 4, 0)

    key_proj = value_proj = None
    for k in range(slices):
        x = x_refs[k][...].reshape(-1, width).astype(jnp.float32)
        slice_at = tensor_at ^ k
        at = pl.ds(pl.multiple_of(slice_at * width, width), width)
        normed = (x * scale * gain_ref[:, at]).astype(jnp.bfloat16)
        wk = wk_ref[slice_at].reshape(width, -1)
        wv = wv_ref[slice_at].reshape(width, -1)
        kp = jnp.dot(normed, wk, preferred_element_type=jnp.float32)
        vp = jnp.dot(normed, wv, preferred_element_type=jnp.float32)
        key_proj = kp if key_proj is None else key_proj + kp
        value_proj = vp if value_proj is None else value_proj + vp
    first = lax.broadcasted_iota(jnp.int32, (heads, 1), 0) < heads // 2
    positions = lax.broadcasted_iota(jnp.int32, (1, slots), 1)
    keys = []
    for h in range(2):
        key = key_proj[:, h * HEAD_DIM : (h + 1) * HEAD_DIM]
        keys.append((rms_rows(key) * kg_ref[...]).astype(jnp.bfloat16))
    value = value_proj.astype(jnp.bfloat16)
    for j in range(per_step):
        seq = step_at * per_step + j
        own = slice(j * slots, (j + 1) * slots)
        query = query_ref[pl.ds(seq, heads, stride=8), :]
        query = (rms_rows(query) * qg_ref[...]).astype(jnp.bfloat16)
        scores = [
            lax.dot_general(
                query, key[own], (((1,), (1,)), ((), ())), preferred_element_type=jnp.float32
            )
            for key in keys
        ]
        scores = jnp.where(first, scores[0], scores[1]) / math.sqrt(HEAD_DIM)
        scores = jnp.where(positions < len_ref[seq >> 1, seq & 1], scores, -1e30)
        expo = jnp.exp(scores - jnp.max(scores, axis=-1, keepdims=True))
        weights = (expo / jnp.sum(expo, axis=-1, keepdims=True)).astype(jnp.bfloat16)
        mixed = jnp.dot(weights, value[own], preferred_element_type=jnp.float32)
        out_ref[j] = jnp.where(first, mixed[:, :HEAD_DIM], mixed[:, HEAD_DIM:])


SMEM = pl.BlockSpec(memory_space=pltpu.SMEM)
VMEM = pl.BlockSpec(memory_space=pltpu.VMEM)


def take_last_call(lengths, own):
    seq_count, _, width = own.shape
    return pl.pallas_call(
        take_last_kernel,
        in_specs=[SMEM, pl.BlockSpec(memory_space=pl.ANY)],
        out_specs=VMEM,
        out_shape=jax.ShapeDtypeStruct((seq_count, width), own.dtype),
        scratch_shapes=[
            pltpu.VMEM((seq_count, 16, width), own.dtype),
            pltpu.SemaphoreType.DMA((seq_count,)),
        ],
    )(lengths, own)


def last_rows_call(at, raw, gains):
    seq_count, width = raw[0].shape
    shape = (Z, 16, (Y - 1) * XLO * (width // (XLO * Z)))
    return pl.pallas_call(
        last_rows_kernel,
        in_specs=[SMEM] + [VMEM] * (len(raw) + 1),
        out_specs=VMEM,
        out_shape=jax.ShapeDtypeStruct(shape, jnp.bfloat16),
        scratch_shapes=[
            pltpu.VMEM((len(raw), seq_count, width), jnp.float32),
            pltpu.VMEM(shape, jnp.float32),
        ],
    )(at, *raw, gains)


def second_payload_call(z_all, rest):
    depth, width = rest[0].shape
    tail_rows = (width // HEAD_DIM - 1) * 8
    tail = z_all.shape[1] // 16 - 1
    return pl.pallas_call(
        second_payload_kernel,
        grid=(1,),
        in_specs=[pl.BlockSpec((Z, 16, z_all.shape[2]), lambda i: (0, tail, 0))]
        + [VMEM] * len(rest),
        out_specs=VMEM,
        out_shape=jax.ShapeDtypeStruct((Z, Y * depth + tail_rows + 16, HEAD_DIM), jnp.bfloat16),
        scratch_shapes=[pltpu.VMEM((Z, tail_rows, HEAD_DIM), jnp.float32)],
    )(z_all, *rest)


def kv_attend(at, lengths, slices, pieces, last, corner, gains, heads, qg, kg):
    seq_count, slots, width = slices[0].shape
    model_width = gains.size
    kv_width = 2 * HEAD_DIM
    rows = model_width // (Y * XLO * Z)
    per_step = 2
    x_spec = pl.BlockSpec((per_step, slots, width), lambda step: (step, 0, 0))
    return pl.pallas_call(
        kv_attend_kernel,
        grid=(seq_count // per_step,),
        in_specs=[SMEM, SMEM]
        + [x_spec] * len(slices)
        + [pl.BlockSpec(memory_space=pltpu.HBM)] * (len(pieces) + 2)
        + [VMEM] * 3,
        out_specs=pl.BlockSpec((per_step, heads, HEAD_DIM), lambda step: (step, 0, 0)),
        out_shape=jax.ShapeDtypeStruct((seq_count, heads, HEAD_DIM), jnp.float32),
        scratch_shapes=[pltpu.VMEM((Y, XLO, Z, rows, kv_width), jnp.bfloat16)] * 2
        + [
            pltpu.VMEM((Z, heads * 8, HEAD_DIM), jnp.bfloat16),
            pltpu.VMEM((heads * 8, HEAD_DIM), jnp.float32),
            pltpu.SemaphoreType.DMA((3,)),
        ],
        compiler_params=pltpu.CompilerParams(vmem_limit_bytes=58 * 1024 * 1024),
        cost_estimate=pl.CostEstimate(
            flops=4 * seq_count * slots * model_width * kv_width,
            bytes_accessed=2 * seq_count * slots * model_width + 4 * model_width * kv_width,
            transcendentals=seq_count * heads * slots,
        ),
    )(at, lengths, *slices, *pieces, last, corner, gains, qg, kg)


def body(
    hidden, lengths, norm_gain, q_norm_gain, k_norm_gain, query_weight, key_weight, value_weight
):
    tensor_size = lax.axis_size("tensor")
    tensor_at = lax.axis_index("tensor")
    dp_at = lax.axis_index("dp")
    x_lo_at = (dp_at >> (Z.bit_length() - 1)) & (XLO - 1)
    y_at = dp_at >> ((Z * XLO).bit_length() - 1)
    at = jnp.stack([y_at, x_lo_at, tensor_at]).astype(jnp.int32)

    pair_count, _, seq_slots, width_local = hidden.shape
    seq_count = 2 * pair_count
    own = hidden.reshape(seq_count, seq_slots, width_local)
    rows_local, kv_width = key_weight.shape
    query_width = query_weight.shape[1]
    gains = norm_gain[None]

    kv_weight = jnp.concatenate([key_weight, value_weight], axis=1)
    kv_both = jnp.concatenate([kv_weight, swap_x_lo(kv_weight)])
    query_other = swap_x_lo(query_weight)
    last_own = take_last_call(lengths, own)
    last_raw = [last_own] + [swap_tensor(last_own, k) for k in range(1, tensor_size)]

    sent_own = lax.optimization_barrier((own, kv_both, query_other, *last_raw))[0]
    far = swap_tensor(sent_own, 2)
    peer = swap_tensor(sent_own, 1)

    block = kv_both[:, : kv_width + HEAD_DIM]
    rows = last_rows_call(at, last_raw, gains)
    rows, _ = lax.optimization_barrier((rows, query_other))
    z_all = exchange(
        jnp.concatenate([jnp.broadcast_to(block[None], (Z,) + block.shape), rows], axis=1),
        Z_GROUPS,
    )

    rest = jnp.concatenate(
        [kv_both[:, kv_width + HEAD_DIM :], jnp.concatenate([query_weight, query_other])], axis=1
    )
    rest = [rest] + [shift(rest, dy=-step) for step in range(1, Y)]

    z_own = lax.optimization_barrier((z_all[:, : block.shape[0]], *rest))[0]
    z_up = shift(z_own, dy=-1)
    z_down = shift(z_own, dy=1)
    far_low = shift(z_up[: Z // 2], dy=-1)
    far_high = shift(z_down[Z // 2 :], dy=1)
    pieces = [z_own, z_up, z_down, far_low, far_high]

    corner = swap_tensor(z_own[0, :16], 1)
    second, corner = lax.optimization_barrier((second_payload_call(z_all, rest), corner))
    last = exchange(second, Z_GROUPS)
    far_peer = swap_tensor(lax.optimization_barrier((far, z_up, z_down))[0], 1)

    mixed = kv_attend(
        at,
        lengths,
        [own, peer, far, far_peer],
        pieces,
        last,
        corner,
        gains,
        query_width // HEAD_DIM,
        q_norm_gain[None],
        k_norm_gain[None],
    ).reshape(seq_count, width_local)

    sent = mixed.astype(jnp.bfloat16)
    near = exchange(jnp.broadcast_to(sent[None], (XLO * Z,) + sent.shape), XZ_GROUPS)
    every = exchange(jnp.broadcast_to(near[None], (Y,) + near.shape), Y_GROUPS)
    every = every.reshape(-1, 2, width_local)
    dots = jnp.dot(every[:, 0], every[:, 1].T, preferred_element_type=jnp.float32)
    every_f32 = every.astype(jnp.float32)
    norms = jnp.sum(every_f32 * every_f32, axis=-1).T
    part = jnp.concatenate([dots, norms], axis=0)
    parts = [part] + [swap_tensor(part, k) for k in range(1, tensor_size)]
    total = (parts[0] + parts[1]) + (parts[2] + parts[3])
    pairs = dots.shape[0]
    scales = lax.rsqrt(total[pairs:] + EPS)
    sim = SCORE_SCALE * total[:pairs] * scales[0][:, None] * scales[1][None, :]
    row_lse = jax.nn.logsumexp(sim, axis=1)
    col_lse = jax.nn.logsumexp(sim, axis=0)
    positive = jnp.sum(jnp.where(jnp.eye(pairs, dtype=bool), sim, 0.0), axis=0)
    all_loss = 0.5 * (row_lse + col_lse) - positive
    loss = jnp.mean(all_loss)
    pair_loss = lax.dynamic_slice_in_dim(all_loss, dp_at * pair_count, pair_count)
    own_scale = lax.dynamic_slice_in_dim(scales, dp_at * pair_count, pair_count, axis=1)
    embeddings = (mixed.reshape(pair_count, 2, width_local) * own_scale.T[:, :, None]).astype(
        jnp.bfloat16
    )
    return (embeddings, pair_loss, loss)


def solution(mesh):
    in_specs = (
        P("dp", None, None, "tensor"),
        P("dp", None),
        P(),
        P(),
        P(),
        P("dp", "tensor"),
        P("dp", "tensor"),
        P("dp", "tensor"),
    )
    out_specs = (P("dp", None, "tensor"), P("dp"), P())
    return jax.shard_map(body, mesh=mesh, in_specs=in_specs, out_specs=out_specs, check_vma=False)
```
